128 devices in a mesh: section: 2 (over z_lo), dp: 8 (over x, core), tensor: 8 (over y, z_hi).
Axes of the slice: x: 4, y: 4, z: 4 (z_hi: 2, z_lo: 2; z = z_hi * 2 + z_lo), core: 2. Of those that a mesh axis runs over, the one named last changes fastest.
Arguments:
- tokens: bfloat16 [256, 12288], P('tensor', 'dp'), may hold values from -6 to 6
- out_grad: bfloat16 [256, 12288], P('tensor', 'dp'), may hold values from -6 to 6
- norm_gain: float32 [2, 12288], P('section'), may hold values from 0.1 to 1.9
- norm_shift: float32 [2, 12288], P('section'), may hold values from -3 to 3
- up_weight: bfloat16 [2, 12288, 24576], P('section', 'dp', 'tensor'), may hold values from -0.0546875 to 0.0546875
- up_bias: float32 [2, 24576], P('section'), may hold values from -3 to 3
- down_weight: bfloat16 [2, 24576, 12288], P('section', 'tensor', 'dp'), may hold values from -0.0390625 to 0.0390625
- down_bias: float32 [2, 12288], P('section'), may hold values from -3 to 3
Outputs:
- segment_output: bfloat16 [2, 256, 12288], P('section', 'tensor', 'dp')
- segment_input_grad: bfloat16 [2, 256, 12288], P('section', 'tensor', 'dp')
The draws below stay inside these ranges and needn't reach their ends.
All inputs are finite; a program needn't handle non-finite values.
Results may differ from the reference program's by a relative error of at most 0.0095.
Values may be sent and summed in bfloat16 or wider, within the bound.
A program may use at most 128 MiB of HBM per device.

```python
import jax
import jax.numpy as jnp
from jax import lax

D = 12288
HIDDEN_SIZE = 24576
TOKENS = 256
N_DP = 8


def block_scale(stream_key, dims, cuts, smallest, largest):
    level, own = 1.0, jax.random.fold_in(stream_key, 6)
    for dim, blocks in cuts:
        steps = jnp.exp(jax.random.uniform(jax.random.fold_in(own, dim), (blocks,), jnp.float32, smallest / len(cuts), largest / len(cuts)))
        level = level * jnp.repeat(steps, dims[dim] // blocks).reshape([-1 if axis == dim else 1 for axis in range(len(dims))])
    return level


def scatter_about(key, dims, deviation, reach, shards=(), held_as=jnp.bfloat16):
    level = block_scale(key, dims, shards, -0.22, 0.18) if shards else 1.0
    entries = jax.random.normal(key, dims, jnp.float32) * deviation * level
    return jnp.minimum(jnp.maximum(entries, -reach), reach).astype(held_as)


def setup_inputs(seed: int = 0) -> dict:
    keys = jax.random.split(jax.random.key(seed), 9)
    return {
        "tokens": scatter_about(keys[0], (TOKENS, D), 1.0, 6.0, ((0, 8), (1, 8))),
        "out_grad": scatter_about(keys[1], (TOKENS, D), 1.0, 6.0, ((0, 8), (1, 8))),
        "norm_gain": jnp.clip(1.0 + 0.18 * jax.random.normal(keys[2], (2, D), jnp.float32), 0.1, 1.9),
        "norm_shift": scatter_about(keys[3], (2, D), 0.5, 3.0, ((0, 2),), jnp.float32),
        "up_weight": scatter_about(keys[4], (2, D, HIDDEN_SIZE), D ** -0.5, 0.0546875, ((0, 2), (1, 8), (2, 8))),
        "up_bias": scatter_about(keys[5], (2, HIDDEN_SIZE), 0.5, 3.0, ((0, 2),), jnp.float32),
        "down_weight": scatter_about(keys[6], (2, HIDDEN_SIZE, D), HIDDEN_SIZE ** -0.5, 0.0390625, ((0, 2), (1, 8), (2, 8))),
        "down_bias": scatter_about(keys[7], (2, D), 0.5, 3.0, ((0, 2),), jnp.float32),
    }


epsilon = 1e-05
root_scale = 0.7978845608028654
cubic_term = 0.044715

def gelu_value(pre_act):
    inner = root_scale * (pre_act + cubic_term * pre_act * pre_act * pre_act)
    return 0.5 * pre_act * (1.0 + jnp.tanh(inner))

def gelu_slope(pre_act):
    inner = root_scale * (pre_act + cubic_term * pre_act * pre_act * pre_act)
    tangent = jnp.tanh(inner)
    return 0.5 * (1.0 + tangent) + 0.5 * pre_act * (1.0 - tangent * tangent) * root_scale * (1.0 + 3.0 * cubic_term * pre_act * pre_act)

def grid_swap(matrix):
    count_rows, count_cols = matrix.shape
    grid = N_DP
    blocks = matrix.reshape(grid, count_rows // grid, grid, count_cols // grid)
    return blocks.transpose(2, 1, 0, 3).reshape(count_rows, count_cols)

def store_layout(values):
    grid = N_DP
    count_rows, count_cols = values.shape
    pieces = values.reshape(grid, grid, count_rows // (grid * grid), grid, count_cols // grid)
    return pieces.transpose(3, 0, 2, 1, 4).reshape(count_rows, count_cols)

def load_layout(stored):
    grid = N_DP
    count_rows, count_cols = stored.shape
    pieces = stored.reshape(grid, grid, count_rows // (grid * grid), grid, count_cols // grid)
    return pieces.transpose(1, 3, 2, 0, 4).reshape(count_rows, count_cols)

def forward(activations, gain_row, shift_row, up_matrix, up_row, down_matrix, down_row):
    as_float = activations.astype(jnp.float32)
    average = lax.optimization_barrier(jnp.mean(as_float, axis=1, keepdims=True))
    centered = as_float - average
    variance = lax.optimization_barrier(jnp.mean(centered * centered, axis=1, keepdims=True))
    inverse_dev = lax.rsqrt(variance + epsilon)
    unit_rows = centered * inverse_dev
    normalized = (unit_rows * gain_row + shift_row).astype(jnp.bfloat16)
    pre_act = jnp.dot(normalized, up_matrix, preferred_element_type=jnp.float32) + up_row
    hidden = gelu_value(pre_act).astype(jnp.bfloat16)
    mixed = jnp.dot(hidden, down_matrix, preferred_element_type=jnp.float32)
    output = (as_float + mixed + down_row).astype(jnp.bfloat16)
    return (output, pre_act, unit_rows, inverse_dev)

def backward(incoming, pre_act, unit_rows, inverse_dev, gain_row, up_matrix, down_matrix):
    hidden_grad = jnp.dot(incoming, down_matrix.T, preferred_element_type=jnp.float32)
    pre_grad = (hidden_grad * gelu_slope(pre_act)).astype(jnp.bfloat16)
    norm_grad = jnp.dot(pre_grad, up_matrix.T, preferred_element_type=jnp.float32)
    scaled = norm_grad * gain_row
    first_mean = lax.optimization_barrier(jnp.mean(scaled, axis=1, keepdims=True))
    second_mean = lax.optimization_barrier(jnp.mean(scaled * unit_rows, axis=1, keepdims=True))
    result = incoming.astype(jnp.float32) + inverse_dev * (scaled - first_mean - unit_rows * second_mean)
    return result.astype(jnp.bfloat16)

def reference(tokens, out_grad, norm_gain, norm_shift, up_weight, up_bias, down_weight, down_bias):
    second_up = grid_swap(up_weight[1])
    second_down = grid_swap(down_weight[1])
    first_out, first_pre, first_unit, first_inv = forward(tokens, norm_gain[0], norm_shift[0], up_weight[0], up_bias[0], down_weight[0], down_bias[0])
    second_out, second_pre, second_unit, second_inv = forward(first_out, norm_gain[1], norm_shift[1], second_up, up_bias[1], second_down, down_bias[1])
    second_grad = backward(load_layout(out_grad), second_pre, second_unit, second_inv, norm_gain[1], second_up, second_down)
    first_grad = backward(second_grad, first_pre, first_unit, first_inv, norm_gain[0], up_weight[0], down_weight[0])
    return (jnp.stack([first_out, store_layout(second_out)]), jnp.stack([first_grad, store_layout(second_grad)]))
```

```python
import functools

import jax
import jax.numpy as jnp
from jax import lax
from jax.experimental import pallas as pl
from jax.experimental.pallas import tpu as pltpu
from jax.sharding import PartitionSpec as P

D = 12288
ROWS = 32
MODEL = 1536
UNITS = 3072
N_CHUNKS, N_WIDTH = 3, 1024
M_CHUNKS, M_WIDTH = 3, 512
MESH = pl.DeviceIdType.MESH
F32, BF16 = jnp.float32, jnp.bfloat16

epsilon = 1e-05
root_scale = 0.7978845608028654
cubic_term = 0.044715


def gelu_value(pre_act):
    inner = root_scale * (pre_act + cubic_term * pre_act * pre_act * pre_act)
    return 0.5 * pre_act * (1.0 + jnp.tanh(inner))


def gelu_slope(pre_act):
    inner = root_scale * (pre_act + cubic_term * pre_act * pre_act * pre_act)
    tangent = jnp.tanh(inner)
    return 0.5 * (1.0 + tangent) + 0.5 * pre_act * (1.0 - tangent * tangent) * root_scale * (
        1.0 + 3.0 * cubic_term * pre_act * pre_act
    )


SEM_NAMES = {}


def sem_index(name, count=1):
    if name not in SEM_NAMES:
        SEM_NAMES[name] = sum(width for _, width in SEM_NAMES.values()), count
    return SEM_NAMES[name][0]


SEM_COUNT = 160


class Group:
    def __init__(self, section, axis, d, t):
        self.axis, self.section, self.d, self.t = axis, section, d, t
        self.index = d if axis == "dp" else t
        self.hi, self.lo = self.index // 2, self.index % 2

    def member(self, index):
        if self.axis == "dp":
            return (self.section, index, self.t)
        return (self.section, self.d, index)

    def at(self, hi, lo):
        return self.member(hi * 2 + lo)

    def pair(self):
        return self.at(self.hi, 1 - self.lo)


class Links:
    def __init__(self, sems):
        self.sems = sems
        self.sent = []

    def sem(self, name, offset=0, count=1):
        return self.sems.at[sem_index(name, count) + offset]

    def send(self, src, dst, to, send_sem, recv_sem):
        pltpu.make_async_remote_copy(
            src_ref=src, dst_ref=dst, send_sem=send_sem, recv_sem=recv_sem,
            device_id=to, device_id_type=MESH,
        ).start()

    def wait_recv(self, ref, sem, peer):
        pltpu.make_async_remote_copy(
            src_ref=ref, dst_ref=ref, send_sem=sem, recv_sem=sem,
            device_id=peer, device_id_type=MESH,
        ).wait_recv()

    def later(self, ref, sem, peer):
        self.sent.append((ref, sem, peer))

    def finish(self):
        for ref, sem, peer in self.sent:
            pltpu.make_async_remote_copy(
                src_ref=ref, dst_ref=ref, send_sem=sem, recv_sem=sem,
                device_id=peer, device_id_type=MESH,
            ).wait_send()
        self.sent = []


class Scatter:
    def __init__(self, links, group, name, part, from_pair, pair_sum, from_four):
        self.links, self.group, self.name = links, group, name
        self.part, self.from_pair, self.pair_sum, self.from_four = part, from_pair, pair_sum, from_four

    def send_pair(self, c):
        g, k = self.group, self.links
        src = self.part.at[c, :, 1 - g.lo]
        sem = k.sem(f"{self.name}/pair_send{c}")
        k.send(src, self.from_pair.at[c], g.pair(), sem, k.sem(f"{self.name}/pair_recv{c}"))
        k.later(src, sem, g.pair())

    def middle(self, c):
        g, k = self.group, self.links
        k.wait_recv(self.from_pair.at[c], k.sem(f"{self.name}/pair_recv{c}"), g.pair())
        total = self.part[c, :, g.lo].astype(F32) + self.from_pair[c].astype(F32)
        self.pair_sum[c] = total.astype(BF16)
        send_sem = k.sem(f"{self.name}/four_send{c}")
        for step in (2, 1, 3):
            to = (g.hi + step) % 4
            k.send(
                self.pair_sum.at[c, to], self.from_four.at[c, step - 1], g.at(to, g.lo),
                send_sem, k.sem(f"{self.name}/four_recv{c}"),
            )
        k.later(self.from_four.at[c], send_sem, g.pair())

    def finish(self, c):
        g, k = self.group, self.links
        k.wait_recv(self.from_four.at[c], k.sem(f"{self.name}/four_recv{c}"), g.pair())
        total = self.part[c, g.hi, g.lo].astype(F32) + self.from_pair[c, g.hi].astype(F32)
        for step in range(3):
            total = total + self.from_four[c, step].astype(F32)
        return total


class Gather:
    def __init__(self, links, group, name, whole):
        self.links, self.group, self.name, self.whole = links, group, name, whole

    def send(self, c):
        g, k = self.group, self.links
        own = self.whole.at[c, g.hi, g.lo]
        send_sem = k.sem(f"{self.name}/own_send{c}")
        for step in (2, 1, 3):
            k.send(own, own, g.at((g.hi + step) % 4, g.lo), send_sem,
                   k.sem(f"{self.name}/four_recv{c}", step - 1, 3))
        k.send(own, own, g.pair(), send_sem, k.sem(f"{self.name}/pair_recv{c}"))
        k.later(self.whole.at[c, :, g.lo], send_sem, g.pair())

    def forward(self, c):
        g, k = self.group, self.links
        send_sem = k.sem(f"{self.name}/on_send{c}")
        for step in (1, 3, 2):
            block = self.whole.at[c, (g.hi + 4 - step) % 4, g.lo]
            k.wait_recv(block, k.sem(f"{self.name}/four_recv{c}", step - 1, 3), g.pair())
            k.send(block, block, g.pair(), send_sem, k.sem(f"{self.name}/pair_recv{c}"))
        k.later(self.whole.at[c, pl.ds(0, 3), g.lo], send_sem, g.pair())

    def ready(self, c):
        g, k = self.group, self.links
        k.wait_recv(self.whole.at[c, :, 1 - g.lo], k.sem(f"{self.name}/pair_recv{c}"), g.pair())


class Cross:
    def __init__(self, links, group, name, whole, partners):
        self.links, self.group, self.name, self.whole, self.partners = links, group, name, whole, partners

    def send(self, source, four):
        g, k = self.group, self.links
        send_sem = k.sem(f"{self.name}/send")
        for to in self.partners:
            k.send(source, self.whole.at[g.hi, g.lo], to, send_sem, k.sem(f"{self.name}/recv", g.hi, 4))
        k.later(four, send_sem, g.pair())

    def receive(self):
        g, k = self.group, self.links
        send_sem = k.sem(f"{self.name}/on_send")
        for hi in range(4):
            block = self.whole.at[hi, g.lo]
            k.wait_recv(block, k.sem(f"{self.name}/recv", hi, 4), g.pair())
            k.send(block, block, g.pair(), send_sem, k.sem(f"{self.name}/pair_recv"))
        k.later(self.whole.at[:, g.lo], send_sem, g.pair())

    def ready(self):
        g, k = self.group, self.links
        k.wait_recv(self.whole.at[:, 1 - g.lo], k.sem(f"{self.name}/pair_recv"), g.pair())


def exchange(links, group, name, table):
    send_sem, recv_sem = links.sem(f"{name}/send"), links.sem(f"{name}/recv")
    for step in (4, 3, 5, 2, 6, 7, 1):
        links.send(table.at[0], table.at[step], group.member((group.index + step) % 8), send_sem, recv_sem)
    links.later(table.at[pl.ds(1, 7)], send_sem, group.pair())


def exchanged(links, group, name, table):
    links.wait_recv(table.at[pl.ds(1, 7)], links.sem(f"{name}/recv"), group.pair())


def two_lanes(first, second):
    lane = lax.broadcasted_iota(jnp.int32, (ROWS, 128), 1)
    return jnp.where(lane < 64, first, second)


def local_moments(values):
    average = jnp.sum(values, 1, keepdims=True) / MODEL
    centered = values - average
    return two_lanes(average, jnp.sum(centered * centered, 1, keepdims=True))


def combined_moments(table):
    average = table[0][:, 0:1]
    squares = table[0][:, 64:65]
    for k in range(1, 8):
        average = average + table[k][:, 0:1]
        squares = squares + table[k][:, 64:65]
    average = average / 8.0
    for k in range(8):
        offset = table[k][:, 0:1] - average
        squares = squares + MODEL * (offset * offset)
    return average, lax.rsqrt(squares / D + epsilon)


def added_lanes(table):
    total = table[0]
    for k in range(1, 8):
        total = total + table[k]
    return total[:, 0:1], total[:, 64:65]


def swap_matrix():
    row = lax.broadcasted_iota(jnp.int32, (256, 256), 0)
    column = lax.broadcasted_iota(jnp.int32, (256, 256), 1)
    source = ((row // 4) % 8) * 32 + (row // 32) * 4 + row % 4
    return jnp.where(column == source, 1.0, 0.0).astype(BF16)


def pick_matrix(q):
    row = lax.broadcasted_iota(jnp.int32, (ROWS, 256), 0)
    column = lax.broadcasted_iota(jnp.int32, (ROWS, 256), 1)
    return jnp.where(column == (row // 4) * 32 + q * 4 + row % 4, 1.0, 0.0)


def product(x, w_ref, transposed, k0, depth, n0, width):
    if transposed:
        return lax.dot_general(
            x, w_ref[pl.ds(n0, width), pl.ds(k0, depth)], (((1,), (1,)), ((), ())),
            preferred_element_type=F32,
        )
    return jnp.dot(x, w_ref[pl.ds(k0, depth), pl.ds(n0, width)], preferred_element_type=F32)


def kernel(
    tokens, out_grad, gain, shift, up, up_bias, down, down_bias, out_ref, grad_ref,
    U, V, gain_row, shift_row, up_row, down_row, xall, xn, xn2, part, from_pair, pair_sum, from_four,
    hall, acc, part_m, from_pair_m, pair_sum_m, from_four_m, pre, hidden_grad, moments, stats, sendbuf,
    own_stats, sems, local_sems,
):
    s, d, t = lax.axis_index("section"), lax.axis_index("dp"), lax.axis_index("tensor")

    barrier = pltpu.get_barrier_semaphore()
    cross_dp = jnp.where(s == 0, t % 2, t)
    cross_tensor = jnp.where(s == 0, d, d % 2)
    step_dp = jnp.where(s == 0, 2, 0)
    partners = [(1 - s, cross_dp + step_dp * k, cross_tensor + (2 - step_dp) * k) for k in range(4)]
    for k in range(1, 8):
        pl.semaphore_signal(barrier, inc=1, device_id=(s, (d + k) % 8, t), device_id_type=MESH)
        pl.semaphore_signal(barrier, inc=1, device_id=(s, d, (t + k) % 8), device_id_type=MESH)
    for to in partners:
        pl.semaphore_signal(barrier, inc=1, device_id=to, device_id_type=MESH)

    def fetch(src, dst, index):
        copy = pltpu.make_async_copy(src, dst, local_sems.at[index])
        copy.start()
        return copy

    def branch(section):
        first = section == 0
        links = Links(sems)
        hidden_group = Group(section, "dp" if first else "tensor", d, t)
        model_group = Group(section, "tensor" if first else "dp", d, t)
        width_index, unit_index = (d, t) if first else (t, d)
        features = pl.ds(pl.multiple_of(width_index * MODEL, MODEL), MODEL)
        units = pl.ds(pl.multiple_of(unit_index * UNITS, UNITS), UNITS)
        g = model_group
        own_x = xall.at[0, 0, g.hi, g.lo]
        get_own = fetch(tokens if first else out_grad, own_x, 0)
        weights = [(up.at[0], U, 1), (down.at[0], V, 2)]
        gets = {}
        for src, dst, index in weights if first else weights[::-1]:
            gets[index] = fetch(src, dst, index)
        small = [
            fetch(gain.at[:, features], gain_row, 3), fetch(shift.at[:, features], shift_row, 4),
            fetch(up_bias.at[:, units], up_row, 5), fetch(down_bias.at[:, features], down_row, 6),
        ]
        get_own.wait()
        pl.semaphore_wait(barrier, 18)

        def scatter_hidden(slot):
            return Scatter(links, hidden_group, f"h{slot}", part.at[slot], from_pair.at[slot],
                           pair_sum.at[slot], from_four.at[slot])

        def scatter_model(slot):
            return Scatter(links, model_group, f"m{slot}", part_m.at[slot], from_pair_m.at[slot],
                           pair_sum_m.at[slot], from_four_m.at[slot])

        def gather_hidden(slot):
            return Gather(links, hidden_group, f"g{slot}", hall.at[slot])

        def start_hidden(x_ref, w_ref, transposed, scatter):
            for c in range(N_CHUNKS):
                @pl.loop(0, N_WIDTH // 512)
                def _(n):
                    at = pl.multiple_of(n * 512, 512)
                    x = x_ref[...].reshape(256, MODEL)
                    value = product(x, w_ref, transposed, 0, MODEL, pl.multiple_of(c * N_WIDTH + n * 512, 512), 512)
                    scatter.part[c, :, :, :, pl.ds(at, 512)] = value.astype(BF16).reshape(4, 2, ROWS, 512)

                scatter.send_pair(c)
                if c >= 1:
                    scatter.middle(c - 1)
            scatter.middle(N_CHUNKS - 1)

        def to_model(gather, c, w_ref, transposed, scatter):
            gather.ready(c)
            if c < N_CHUNKS - 1:
                @pl.loop(0, MODEL // 512)
                def _(n):
                    at = pl.multiple_of(n * 512, 512)
                    x = gather.whole[c].reshape(256, N_WIDTH)
                    value = product(x, w_ref, transposed, c * N_WIDTH, N_WIDTH, at, 512)
                    if c == 0:
                        acc[:, pl.ds(at, 512)] = value
                    else:
                        acc[:, pl.ds(at, 512)] += value
                return
            for m in range(M_CHUNKS):
                at = m * M_WIDTH
                x = gather.whole[c].reshape(256, N_WIDTH)
                value = product(x, w_ref, transposed, c * N_WIDTH, N_WIDTH, at, M_WIDTH)
                value = value + acc[:, pl.ds(at, M_WIDTH)]
                scatter.part[m] = value.astype(BF16).reshape(4, 2, ROWS, M_WIDTH)
                scatter.send_pair(m)
                if m >= 1:
                    scatter.middle(m - 1)
            scatter.middle(M_CHUNKS - 1)

        def through(scatter, gather, epilogue, w_ref, transposed, scatter_out):
            for c in range(N_CHUNKS):
                if scatter is None:
                    value = epilogue(c, None)
                else:
                    value = epilogue(c, scatter.finish(c))
                gather.whole[c, hidden_group.hi, hidden_group.lo] = value.astype(BF16)
                gather.send(c)
                if c >= 1:
                    gather.forward(c - 1)
                if c >= 2:
                    to_model(gather, c - 2, w_ref, transposed, scatter_out)
            gather.forward(N_CHUNKS - 1)
            to_model(gather, N_CHUNKS - 2, w_ref, transposed, scatter_out)
            to_model(gather, N_CHUNKS - 1, w_ref, transposed, scatter_out)

        def finish_model(scatter):
            return jnp.concatenate([scatter.finish(m) for m in range(M_CHUNKS)], axis=1)

        def normalize_all(source):
            for hi in range(4):
                for lo in range(2):
                    average = stats[hi, lo][:, 0:1]
                    inverse_dev = stats[hi, lo][:, 64:65]
                    unit = (source[hi, lo].astype(F32) - average) * inverse_dev
                    xn[hi, lo] = (unit * gain_row[...] + shift_row[...]).astype(BF16)

        def unit_slice(c):
            return pl.ds(c * N_WIDTH, N_WIDTH)

        def input_gradient(incoming, norm_grad, unit, inverse_dev, slot):
            scaled = norm_grad * gain_row[...]
            group = hidden_group
            moments[slot, 0] = two_lanes(
                jnp.sum(scaled, 1, keepdims=True), jnp.sum(scaled * unit, 1, keepdims=True)
            )
            exchange(links, group, "sums", moments.at[slot])
            exchanged(links, group, "sums", moments.at[slot])
            first_sum, second_sum = added_lanes(moments.at[slot])
            return (incoming + inverse_dev * (scaled - first_sum / D - unit * (second_sum / D))).astype(BF16)

        tokens_gather = Gather(links, model_group, "x", xall.at[0])
        rows_across = Cross(links, model_group, "y0" if first else "g1", xall.at[1, 0], partners)
        rows_back = Cross(links, model_group, "g1" if first else "y0", xall.at[1, 0], partners)
        stats_cross = Cross(links, model_group, "y0stats", stats, partners)

        tokens_gather.send(0)
        if first:
            own = own_x[...].astype(F32)
            moments[0, 0] = local_moments(own)
            exchange(links, hidden_group, "0first", moments.at[0])
            exchanged(links, hidden_group, "0first", moments.at[0])
            average, inverse_dev = combined_moments(moments.at[0])
            own_stats[...] = two_lanes(average, inverse_dev)
            stats[g.hi, g.lo] = own_stats[...]
            for k in range(1, 8):
                place = stats.at[g.hi, g.lo]
                links.send(place, place, g.member((g.index + k) % 8), links.sem("0st/send"), links.sem("0st/recv"))
            links.later(moments.at[0, pl.ds(0, 7)], links.sem("0st/send"), g.pair())
            tokens_gather.forward(0)
            tokens_gather.ready(0)
            links.wait_recv(moments.at[0, pl.ds(0, 7)], links.sem("0st/recv"), g.pair())
            for copy in small:
                copy.wait()
            normalize_all(xall.at[0, 0])
            gets[1].wait()
            scatter = scatter_hidden(0)
            start_hidden(xn, U, False, scatter)
            gets[2].wait()

            def forward_hidden(c, value):
                value = value + up_row[:, unit_slice(c)]
                pre[:, unit_slice(c)] = value
                return gelu_value(value)

            scatter_out = scatter_model(0)
            through(scatter, gather_hidden(0), forward_hidden, V, False, scatter_out)
            mixed = finish_model(scatter_out)
            y0 = (own_x[...].astype(F32) + mixed + down_row[...]).astype(BF16)
            sendbuf[0] = y0
            rows_across.send(sendbuf.at[0], sendbuf)
            moments[1, 0] = local_moments(y0.astype(F32))
            exchange(links, hidden_group, "0second", moments.at[1])
            out_ref[0] = y0
            exchanged(links, hidden_group, "0second", moments.at[1])
            average, inverse_dev = combined_moments(moments.at[1])
            moments[3, 0] = two_lanes(average, inverse_dev)
            stats_cross.send(moments.at[3, 0], moments.at[3, pl.ds(0, 4)])

            rows_back.receive()
            rows_back.ready()
            xn2[...] = jnp.dot(
                swap_matrix(), xall[1, 0].reshape(256, MODEL), preferred_element_type=F32
            ).astype(BF16).reshape(4, 2, ROWS, MODEL)
            scatter = scatter_hidden(1)
            start_hidden(xn2, V, True, scatter)

            def backward_hidden(c, value):
                return value * gelu_slope(pre[:, unit_slice(c)])

            scatter_out = scatter_model(1)
            through(scatter, gather_hidden(1), backward_hidden, U, True, scatter_out)
            norm_grad = finish_model(scatter_out)
            average, inverse_dev = own_stats[:, 0:1], own_stats[:, 64:65]
            unit = (own_x[...].astype(F32) - average) * inverse_dev
            incoming = xn2[g.hi, g.lo].astype(F32)
            grad_ref[0] = input_gradient(incoming, norm_grad, unit, inverse_dev, 2)
        else:
            tokens_gather.forward(0)
            tokens_gather.ready(0)
            gets[2].wait()
            scatter = scatter_hidden(0)
            start_hidden(xall.at[0, 0], V, True, scatter)
            for c in range(N_CHUNKS):
                hidden_grad[:, unit_slice(c)] = scatter.finish(c)
            for copy in small:
                copy.wait()
            gets[1].wait()

            rows_back.receive()
            stats_cross.receive()
            rows_back.ready()
            stats_cross.ready()
            normalize_all(xall.at[1, 0])
            xn2[...] = jnp.dot(
                swap_matrix(), xn[...].reshape(256, MODEL), preferred_element_type=F32
            ).astype(BF16).reshape(4, 2, ROWS, MODEL)
            scatter = scatter_hidden(1)
            start_hidden(xn2, U, False, scatter)
            pick = pick_matrix(d)
            y0_own = jnp.dot(
                pick.astype(BF16), xall[1, 0].reshape(256, MODEL), preferred_element_type=F32
            )
            own_stats[...] = jnp.dot(
                pick, stats[...].reshape(256, 128), preferred_element_type=F32,
                precision=lax.Precision.HIGHEST,
            )

            def backward_hidden(c, value):
                value = value + up_row[:, unit_slice(c)]
                pre[:, unit_slice(c)] = value
                return hidden_grad[:, unit_slice(c)] * gelu_slope(value)

            scatter_out = scatter_model(0)
            through(scatter, gather_hidden(0), backward_hidden, U, True, scatter_out)
            norm_grad = finish_model(scatter_out)
            average, inverse_dev = own_stats[:, 0:1], own_stats[:, 64:65]
            unit = (y0_own - average) * inverse_dev
            g1 = input_gradient(own_x[...].astype(F32), norm_grad, unit, inverse_dev, 2)
            sendbuf[0] = g1
            rows_across.send(sendbuf.at[0], sendbuf)
            grad_ref[0] = g1

            def forward_hidden(c, value):
                return gelu_value(pre[:, unit_slice(c)])

            scatter_out = scatter_model(1)
            through(None, gather_hidden(1), forward_hidden, V, False, scatter_out)
            mixed = finish_model(scatter_out)
            out_ref[0] = (y0_own + mixed + down_row[...]).astype(BF16)
        links.finish()

    for section in range(2):
        pl.when(s == section)(functools.partial(branch, section))
    assert sum(width for _, width in SEM_NAMES.values()) <= SEM_COUNT


def shards(tokens, out_grad, norm_gain, norm_shift, up_weight, up_bias, down_weight, down_bias):
    vmem = pltpu.VMEM
    return pl.pallas_call(
        kernel,
        out_shape=[jax.ShapeDtypeStruct((1, ROWS, MODEL), BF16)] * 2,
        in_specs=[pl.BlockSpec(memory_space=pl.ANY)] * 8,
        out_specs=[pl.BlockSpec(memory_space=vmem)] * 2,
        scratch_shapes=[
            vmem((MODEL, UNITS), BF16),
            vmem((UNITS, MODEL), BF16),
            vmem((1, MODEL), F32),
            vmem((1, MODEL), F32),
            vmem((1, UNITS), F32),
            vmem((1, MODEL), F32),
            vmem((2, 1, 4, 2, ROWS, MODEL), BF16),
            vmem((4, 2, ROWS, MODEL), BF16),
            vmem((4, 2, ROWS, MODEL), BF16),
            vmem((2, N_CHUNKS, 4, 2, ROWS, N_WIDTH), BF16),
            vmem((2, N_CHUNKS, 4, ROWS, N_WIDTH), BF16),
            vmem((2, N_CHUNKS, 4, ROWS, N_WIDTH), BF16),
            vmem((2, N_CHUNKS, 3, ROWS, N_WIDTH), BF16),
            vmem((2, N_CHUNKS, 4, 2, ROWS, N_WIDTH), BF16),
            vmem((256, MODEL), F32),
            vmem((2, M_CHUNKS, 4, 2, ROWS, M_WIDTH), BF16),
            vmem((2, M_CHUNKS, 4, ROWS, M_WIDTH), BF16),
            vmem((2, M_CHUNKS, 4, ROWS, M_WIDTH), BF16),
            vmem((2, M_CHUNKS, 3, ROWS, M_WIDTH), BF16),
            vmem((ROWS, UNITS), F32),
            vmem((ROWS, UNITS), F32),
            vmem((4, 8, ROWS, 128), F32),
            vmem((4, 2, ROWS, 128), F32),
            vmem((4, ROWS, MODEL), BF16),
            vmem((ROWS, 128), F32),
            pltpu.SemaphoreType.DMA((SEM_COUNT,)),
            pltpu.SemaphoreType.DMA((8,)),
        ],
        compiler_params=pltpu.CompilerParams(
            collective_id=0, has_side_effects=True, vmem_limit_bytes=58 * 2**20
        ),
        cost_estimate=pl.CostEstimate(flops=10**10, bytes_accessed=2 * 10**7, transcendentals=10**5),
        name="relay",
    )(tokens, out_grad, norm_gain, norm_shift, up_weight, up_bias, down_weight, down_bias)


def solution(mesh):
    placed = (
        P("tensor", "dp"),
        P("tensor", "dp"),
        P("section", None),
        P("section", None),
        P("section", "dp", "tensor"),
        P("section", None),
        P("section", "tensor", "dp"),
        P("section", None),
    )
    return jax.shard_map(
        shards,
        mesh=mesh,
        in_specs=placed,
        out_specs=(P("section", "tensor", "dp"), P("section", "tensor", "dp")),
        check_vma=False,
    )
```

```python
import functools

import jax
import jax.numpy as jnp
from jax import lax
from jax.experimental import pallas as pl
from jax.experimental.pallas import tpu as pltpu
from jax.sharding import PartitionSpec as P

D = 12288
ROWS = 32
MODEL = 1536
UNITS = 3072
HALVES = 2
BLOCK = ROWS // HALVES
HALF = 8 * BLOCK
N_CHUNKS, N_WIDTH = 2, 1536
M_CHUNKS, M_WIDTH = 1, 1536
FAR_FIRST = (4, 3, 5, 2, 6, 7, 1)
MESH = pl.DeviceIdType.MESH
F32, BF16 = jnp.float32, jnp.bfloat16

epsilon = 1e-05
root_scale = 0.7978845608028654
cubic_term = 0.044715


def gelu_value(pre_act):
    inner = root_scale * (pre_act + cubic_term * pre_act * pre_act * pre_act)
    return 0.5 * pre_act * (1.0 + jnp.tanh(inner))


def gelu_slope(pre_act):
    inner = root_scale * (pre_act + cubic_term * pre_act * pre_act * pre_act)
    tangent = jnp.tanh(inner)
    return 0.5 * (1.0 + tangent) + 0.5 * pre_act * (1.0 - tangent * tangent) * root_scale * (
        1.0 + 3.0 * cubic_term * pre_act * pre_act
    )


SEM_NAMES = {}


def sem_index(name, count=1):
    if name not in SEM_NAMES:
        SEM_NAMES[name] = sum(width for _, width in SEM_NAMES.values()), count
    return SEM_NAMES[name][0]


SEM_COUNT = 220


class Group:
    def __init__(self, section, axis, d, t):
        self.axis, self.section, self.d, self.t = axis, section, d, t
        self.index = d if axis == "dp" else t
        self.hi, self.lo = self.index // 2, self.index % 2

    def member(self, index):
        if self.axis == "dp":
            return (self.section, index, self.t)
        return (self.section, self.d, index)

    def at(self, hi, lo):
        return self.member(hi * 2 + lo)

    def pair(self):
        return self.at(self.hi, 1 - self.lo)


class Links:
    def __init__(self, sems):
        self.sems = sems
        self.sent = []

    def sem(self, name, offset=0, count=1):
        return self.sems.at[sem_index(name, count) + offset]

    def send(self, src, dst, to, send_sem, recv_sem):
        pltpu.make_async_remote_copy(
            src_ref=src, dst_ref=dst, send_sem=send_sem, recv_sem=recv_sem,
            device_id=to, device_id_type=MESH,
        ).start()

    def wait_recv(self, ref, sem, peer):
        pltpu.make_async_remote_copy(
            src_ref=ref, dst_ref=ref, send_sem=sem, recv_sem=sem,
            device_id=peer, device_id_type=MESH,
        ).wait_recv()

    def later(self, ref, sem, peer):
        self.sent.append((ref, sem, peer))

    def finish(self):
        for ref, sem, peer in self.sent:
            pltpu.make_async_remote_copy(
                src_ref=ref, dst_ref=ref, send_sem=sem, recv_sem=sem,
                device_id=peer, device_id_type=MESH,
            ).wait_send()
        self.sent = []


class PairScatter:
    def __init__(self, links, group, name, part, from_pair, pair_sum, received):
        self.links, self.group, self.name = links, group, name
        self.part, self.from_pair, self.pair_sum = part, from_pair, pair_sum
        self.received = received.at[pl.ds(0, 3)]

    def send(self):
        g, k = self.group, self.links
        src = self.part.at[:, 1 - g.lo]
        sem = k.sem(f"{self.name}/pair_send")
        k.send(src, self.from_pair, g.pair(), sem, k.sem(f"{self.name}/pair_recv"))
        k.later(src, sem, g.pair())

    def middle(self):
        g, k = self.group, self.links
        yield
        k.wait_recv(self.from_pair, k.sem(f"{self.name}/pair_recv"), g.pair())
        total = self.part[:, g.lo].astype(F32) + self.from_pair[...].astype(F32)
        self.pair_sum[...] = total.astype(BF16)
        send_sem = k.sem(f"{self.name}/send")
        for step in (2, 1, 3):
            to = (g.hi + step) % 4
            k.send(self.pair_sum.at[to], self.received.at[step - 1], g.at(to, g.lo), send_sem,
                   k.sem(f"{self.name}/recv"))
        k.later(self.received, send_sem, g.pair())

    def finish(self):
        g, k = self.group, self.links
        k.wait_recv(self.received, k.sem(f"{self.name}/recv"), g.pair())
        total = self.part[g.hi, g.lo].astype(F32) + self.from_pair[g.hi].astype(F32)
        for step in range(3):
            total = total + self.received[step].astype(F32)
        return total


class DirectScatter:
    def __init__(self, links, group, name, part, from_pair, pair_sum, received):
        self.links, self.group, self.name, self.part, self.received = links, group, name, part, received

    def send(self):
        g, k = self.group, self.links
        send_sem = k.sem(f"{self.name}/send")
        for step in FAR_FIRST:
            to = (g.index + step) % 8
            k.send(self.part.at[to // 2, to % 2], self.received.at[step - 1], g.member(to), send_sem,
                   k.sem(f"{self.name}/recv"))
        k.later(self.received, send_sem, g.pair())

    def middle(self):
        return
        yield

    def finish(self):
        g, k = self.group, self.links
        k.wait_recv(self.received, k.sem(f"{self.name}/recv"), g.pair())
        total = self.part[g.hi, g.lo].astype(F32)
        for step in range(7):
            total = total + self.received[step].astype(F32)
        return total


class PairGather:
    def __init__(self, links, group, name, whole, seven):
        self.links, self.group, self.name, self.whole = links, group, name, whole

    def send(self):
        g, k = self.group, self.links
        own = self.whole.at[g.hi, g.lo]
        send_sem = k.sem(f"{self.name}/send")
        for step in (2, 1, 3):
            k.send(own, own, g.at((g.hi + step) % 4, g.lo), send_sem, k.sem(f"{self.name}/recv", step - 1, 3))
        k.send(own, own, g.pair(), send_sem, k.sem(f"{self.name}/pair_recv"))
        k.later(self.whole.at[:, g.lo], send_sem, g.pair())

    def forward(self):
        g, k = self.group, self.links
        send_sem = k.sem(f"{self.name}/on_send")
        yield
        for step in (1, 3, 2):
            block = self.whole.at[(g.hi + 4 - step) % 4, g.lo]
            k.wait_recv(block, k.sem(f"{self.name}/recv", step - 1, 3), g.pair())
            k.send(block, block, g.pair(), send_sem, k.sem(f"{self.name}/pair_recv"))
        k.later(self.whole.at[pl.ds(0, 3), g.lo], send_sem, g.pair())

    def ready(self):
        g, k = self.group, self.links
        k.wait_recv(self.whole.at[:, 1 - g.lo], k.sem(f"{self.name}/pair_recv"), g.pair())


class DirectGather:
    def __init__(self, links, group, name, whole, seven):
        self.links, self.group, self.name, self.whole, self.seven = links, group, name, whole, seven

    def send(self):
        g, k = self.group, self.links
        own = self.whole.at[g.hi, g.lo]
        send_sem = k.sem(f"{self.name}/send")
        for step in FAR_FIRST:
            k.send(own, own, g.member((g.index + step) % 8), send_sem, k.sem(f"{self.name}/recv"))
        k.later(self.seven, send_sem, g.pair())

    def forward(self):
        return
        yield

    def ready(self):
        self.links.wait_recv(self.seven, self.links.sem(f"{self.name}/recv"), self.group.pair())


class Cross:
    def __init__(self, links, group, name, whole, partners):
        self.links, self.group, self.name, self.whole, self.partners = links, group, name, whole, partners

    def send(self, source, four):
        g, k = self.group, self.links
        send_sem = k.sem(f"{self.name}/send")
        for to in self.partners:
            k.send(source, self.whole.at[g.hi, g.lo], to, send_sem, k.sem(f"{self.name}/recv", g.hi, 4))
        k.later(four, send_sem, g.pair())

    def receive(self):
        g, k = self.group, self.links
        send_sem = k.sem(f"{self.name}/on_send")
        yield
        for hi in range(4):
            block = self.whole.at[hi, g.lo]
            k.wait_recv(block, k.sem(f"{self.name}/recv", hi, 4), g.pair())
            k.send(block, block, g.pair(), send_sem, k.sem(f"{self.name}/pair_recv"))
        k.later(self.whole.at[:, g.lo], send_sem, g.pair())

    def ready(self):
        g, k = self.group, self.links
        k.wait_recv(self.whole.at[:, 1 - g.lo], k.sem(f"{self.name}/pair_recv"), g.pair())


def exchange(links, group, name, table, combine):
    send_sem, recv_sem = links.sem(f"{name}/send"), links.sem(f"{name}/recv")
    for step in FAR_FIRST:
        links.send(table.at[0], table.at[step], group.member((group.index + step) % 8), send_sem, recv_sem)
    links.later(table.at[pl.ds(1, 7)], send_sem, group.pair())
    yield
    links.wait_recv(table.at[pl.ds(1, 7)], recv_sem, group.pair())
    return combine([table[k] for k in range(8)])


def pairwise(links, group, name, table, combine):
    pair_send, pair_recv = links.sem(f"{name}/pair_send"), links.sem(f"{name}/pair_recv")
    links.send(table.at[0], table.at[1], group.pair(), pair_send, pair_recv)
    links.later(table.at[0], pair_send, group.pair())
    yield
    links.wait_recv(table.at[1], pair_recv, group.pair())
    table[2] = combine([table[0], table[1]])
    send_sem, recv_sem = links.sem(f"{name}/send"), links.sem(f"{name}/recv")
    for step in (2, 1, 3):
        links.send(table.at[2], table.at[2 + step], group.at((group.hi + step) % 4, group.lo), send_sem, recv_sem)
    links.later(table.at[pl.ds(3, 3)], send_sem, group.pair())
    yield
    links.wait_recv(table.at[pl.ds(3, 3)], recv_sem, group.pair())
    return combine([table[k] for k in range(2, 6)])


def drive(chains):
    alive = list(chains)
    while alive:
        for chain in list(alive):
            try:
                next(chain)
            except StopIteration:
                alive.remove(chain)


def add_all(parts):
    return functools.reduce(lambda left, right: left + right, parts)


def join_moments(parts):
    averages = [part[:, 0:1] for part in parts]
    average = add_all(averages) / len(parts)
    squares = add_all([part[:, 64:65] for part in parts])
    spread = add_all([(one - average) * (one - average) for one in averages])
    return two_lanes(average, squares + (MODEL if len(parts) == 2 else 2 * MODEL) * spread)


def two_lanes(first, second):
    lane = lax.broadcasted_iota(jnp.int32, (BLOCK, 128), 1)
    return jnp.where(lane < 64, first, second)


def local_moments(values):
    average = jnp.sum(values, 1, keepdims=True) / MODEL
    centered = values - average
    return two_lanes(average, jnp.sum(centered * centered, 1, keepdims=True))


def row_stats(joined):
    return two_lanes(joined[:, 0:1], lax.rsqrt(joined[:, 64:65] / D + epsilon))


def selection(rows, columns, source):
    row = lax.broadcasted_iota(jnp.int32, (rows, columns), 0)
    column = lax.broadcasted_iota(jnp.int32, (rows, columns), 1)
    return jnp.where(column == source(row), 1.0, 0.0)


WITHIN = BLOCK // 8


def swap_matrix():
    return selection(HALF, HALF, lambda i: ((i // WITHIN) % 8) * BLOCK + (i // BLOCK) * WITHIN + i % WITHIN).astype(BF16)


def pick_matrix(q):
    return selection(BLOCK, HALF, lambda i: (i // WITHIN) * BLOCK + q * WITHIN + i % WITHIN)


def halves_matrix():
    return selection(ROWS, ROWS, lambda i: ((i % BLOCK) // WITHIN) * 4 + (i // BLOCK) * WITHIN + i % WITHIN).astype(BF16)


def whole_matrix():
    return selection(ROWS, ROWS, lambda i: ((i % 4) // WITHIN) * BLOCK + (i // 4) * WITHIN + i % WITHIN).astype(BF16)


def moved(matrix, rows):
    return jnp.dot(matrix, rows, preferred_element_type=F32).astype(BF16)


def product(x, w_ref, transposed, k0, depth, n0, width):
    if transposed:
        return lax.dot_general(
            x, w_ref[pl.ds(n0, width), pl.ds(k0, depth)], (((1,), (1,)), ((), ())),
            preferred_element_type=F32,
        )
    return jnp.dot(x, w_ref[pl.ds(k0, depth), pl.ds(n0, width)], preferred_element_type=F32)


def kernel(
    tokens, out_grad, gain, shift, up, up_bias, down, down_bias, out_ref, grad_ref,
    U, V, gain_row, shift_row, up_row, down_row, raw, xall, xn, xn2, part, from_pair, pair_sum, received,
    hall, acc, part_m, from_pair_m, pair_sum_m, received_m, pre, hidden_grad, moments, stats, cross_stats,
    sendbuf, gradbuf, y0_own, own_stats, sems, local_sems,
):
    s, d, t = lax.axis_index("section"), lax.axis_index("dp"), lax.axis_index("tensor")

    barrier = pltpu.get_barrier_semaphore()
    greeted = [(s, d + 1 - 2 * (d % 2), t), (1 - s, d, t)]
    greeted += [(s, (d + 2 * k) % 8, t) for k in range(1, 4)]
    greeted += [(s, d, (t + k) % 8) for k in range(1, 8)]
    for to in greeted:
        pl.semaphore_signal(barrier, inc=1, device_id=to, device_id_type=MESH)

    def fetch(src, dst, index):
        copy = pltpu.make_async_copy(src, dst, local_sems.at[index])
        copy.start()
        return copy

    def branch(section):
        first = section == 0
        links = Links(sems)
        hidden_group = Group(section, "dp" if first else "tensor", d, t)
        model_group = Group(section, "tensor" if first else "dp", d, t)
        width_index, unit_index = (d, t) if first else (t, d)
        features = pl.ds(pl.multiple_of(width_index * MODEL, MODEL), MODEL)
        units = pl.ds(pl.multiple_of(unit_index * UNITS, UNITS), UNITS)
        g, hg = model_group, hidden_group
        get_own = fetch(tokens if first else out_grad, raw, 0)
        weights = [(up.at[0], U, 1), (down.at[0], V, 2)]
        gets = {}
        for src, dst, index in weights if first else weights[::-1]:
            gets[index] = fetch(src, dst, index)
        small = [
            fetch(gain.at[:, features], gain_row, 3), fetch(shift.at[:, features], shift_row, 4),
            fetch(up_bias.at[:, units], up_row, 5), fetch(down_bias.at[:, features], down_row, 6),
        ]

        def need(index):
            if index in gets:
                gets.pop(index).wait()

        get_own.wait()
        own_rows = moved(halves_matrix(), raw[...]) if HALVES == 2 else raw[...]
        for h in range(HALVES):
            xall[0, h, g.hi, g.lo] = own_rows[h * BLOCK:(h + 1) * BLOCK]
        for copy in small:
            copy.wait()
        pl.semaphore_wait(barrier, len(greeted))

        def own_x(h):
            return xall[0, h, g.hi, g.lo].astype(F32)

        def scatter_of(group):
            return PairScatter if group.axis == "dp" else DirectScatter

        def gather_of(group):
            return PairGather if group.axis == "dp" else DirectGather

        def scatter_hidden(slot, h):
            return [
                scatter_of(hg)(links, hg, f"h{slot}{h}{c}", part.at[slot, h, c], from_pair.at[slot, h, c],
                               pair_sum.at[slot, h, c], received.at[slot, h, c])
                for c in range(N_CHUNKS)
            ]

        def scatter_model(slot, h):
            return [
                scatter_of(g)(links, g, f"m{slot}{h}{m}", part_m.at[slot, h, m], from_pair_m.at[slot, h, m],
                              pair_sum_m.at[slot, h, m], received_m.at[slot, h, m])
                for m in range(M_CHUNKS)
            ]

        def gather_hidden(slot, h):
            return [gather_of(hg)(links, hg, f"g{slot}{h}{c}", hall.at[slot, h, c], received.at[slot, h, c]) for c in range(N_CHUNKS)]

        def gather_rows(name, slot, h):
            return gather_of(g)(links, g, f"{name}{h}", xall.at[slot, h], received_m.at[slot, h, 0])

        def start_hidden(x_ref, w_ref, transposed, scatters):
            for c, scatter in enumerate(scatters):
                x = x_ref[...].reshape(HALF, MODEL)
                for at in range(0, N_WIDTH, 512):
                    value = product(x, w_ref, transposed, 0, MODEL, c * N_WIDTH + at, 512)
                    scatter.part[:, :, :, pl.ds(at, 512)] = value.astype(BF16).reshape(4, 2, BLOCK, 512)
                scatter.send()
                if c >= 1:
                    yield from scatters[c - 1].middle()
            yield from scatters[-1].middle()

        def to_model(h, gathers, w_ref, transposed, scatters):
            for c, gather in enumerate(gathers):
                yield
                gather.ready()
                x = gather.whole[...].reshape(HALF, N_WIDTH)
                if c < N_CHUNKS - 1:
                    for at in range(0, MODEL, 512):
                        value = product(x, w_ref, transposed, c * N_WIDTH, N_WIDTH, at, 512)
                        acc[h, :, pl.ds(at, 512)] = value if c == 0 else acc[h, :, pl.ds(at, 512)] + value
                    continue
                for m, scatter in enumerate(scatters):
                    for at in range(0, M_WIDTH, 512):
                        value = product(x, w_ref, transposed, c * N_WIDTH, N_WIDTH, m * M_WIDTH + at, 512)
                        if c > 0:
                            value = value + acc[h, :, pl.ds(m * M_WIDTH + at, 512)]
                        scatter.part[:, :, :, pl.ds(at, 512)] = value.astype(BF16).reshape(4, 2, BLOCK, 512)
                    scatter.send()
                    if m >= 1:
                        yield from scatters[m - 1].middle()
            yield from scatters[-1].middle()

        def through(h, scatters, gathers, epilogue, w_ref, transposed, scatters_out):
            for c, scatter in enumerate(scatters):
                yield
                value = epilogue(h, unit_slice(c), scatter.finish())
                gathers[c].whole[hg.hi, hg.lo] = value.astype(BF16)
                gathers[c].send()
                if c >= 1:
                    yield from gathers[c - 1].forward()
            yield from gathers[-1].forward()
            yield from to_model(h, gathers, w_ref, transposed, scatters_out)

        def finish_model(scatters):
            yield
            return jnp.concatenate([scatter.finish() for scatter in scatters], axis=1)

        def normalize_all(h, source):
            for hi in range(4):
                for lo in range(2):
                    average = stats[h, hi, lo][:, 0:1]
                    inverse_dev = stats[h, hi, lo][:, 64:65]
                    unit = (source[hi, lo].astype(F32) - average) * inverse_dev
                    xn[h, hi, lo] = (unit * gain_row[...] + shift_row[...]).astype(BF16)

        def swapped(h, source):
            rows = moved(swap_matrix(), source[...].reshape(HALF, MODEL))
            xn2[h] = rows.reshape(4, 2, BLOCK, MODEL)

        def unit_slice(c):
            return pl.ds(c * N_WIDTH, N_WIDTH)

        def input_gradient(h, incoming, norm_grad, rows):
            average, inverse_dev = own_stats[h][:, 0:1], own_stats[h][:, 64:65]
            unit = (rows - average) * inverse_dev
            scaled = norm_grad * gain_row[...]
            table = moments.at[h, 2]
            table[0] = two_lanes(jnp.sum(scaled, 1, keepdims=True), jnp.sum(scaled * unit, 1, keepdims=True))
            total = yield from (pairwise if first else exchange)(links, hg, f"sums{h}", table, add_all)
            first_mean, second_mean = total[:, 0:1] / D, total[:, 64:65] / D
            return (incoming + inverse_dev * (scaled - first_mean - unit * second_mean)).astype(BF16)

        def store_rows(ref, rows):
            rows = rows[...].reshape(ROWS, MODEL)
            ref[0] = moved(whole_matrix(), rows) if HALVES == 2 else rows

        partners = [(1, 2 * k + t % 2, d) for k in range(4)]

        def y0_cross(h):
            return Cross(links, g, f"y0{h}", xall.at[1, h], partners)

        def stats_cross(h):
            return Cross(links, g, f"y0stats{h}", stats.at[h], partners)

        def transposed_sems(h):
            return links.sem(f"g1{h}/send"), links.sem(f"g1{h}/recv")

        def first_chain(h):
            gather = gather_rows("x", 0, h)
            gather.send()
            moments[h, 0, 0] = local_moments(own_x(h))
            joined = yield from pairwise(links, hg, f"first{h}", moments.at[h, 0], join_moments)
            own_stats[h] = row_stats(joined)
            stats[h, g.hi, g.lo] = own_stats[h]
            stats_gather = DirectGather(links, g, f"st{h}", stats.at[h], moments.at[h, 0, pl.ds(0, 7)])
            stats_gather.send()
            yield
            gather.ready()
            stats_gather.ready()
            normalize_all(h, xall.at[0, h])
            need(1)
            scatters = scatter_hidden(0, h)
            yield from start_hidden(xn.at[h], U, False, scatters)
            need(2)

            def forward_hidden(h, at, value):
                value = value + up_row[:, at]
                pre[h, :, at] = value
                return gelu_value(value)

            scatters_out = scatter_model(0, h)
            yield from through(h, scatters, gather_hidden(0, h), forward_hidden, V, False, scatters_out)
            mixed = yield from finish_model(scatters_out)
            y0 = (own_x(h) + mixed + down_row[...]).astype(BF16)
            sendbuf[0, h] = y0
            y0_cross(h).send(sendbuf.at[0, h], sendbuf.at[pl.ds(0, 4), h])
            moments[h, 1, 0] = local_moments(y0.astype(F32))
            joined = yield from pairwise(links, hg, f"second{h}", moments.at[h, 1], join_moments)
            cross_stats[h, 0] = row_stats(joined)
            stats_cross(h).send(cross_stats.at[h, 0], cross_stats.at[h])
            if h == HALVES - 1:
                store_rows(out_ref, sendbuf.at[0])

            yield
            place = xall.at[1, h, g.hi, g.lo]
            links.wait_recv(place, transposed_sems(h)[1], g.pair())
            gather = gather_rows("g1x", 1, h)
            gather.send()
            yield
            gather.ready()
            swapped(h, xall.at[1, h])
            scatters = scatter_hidden(1, h)
            yield from start_hidden(xn2.at[h], V, True, scatters)

            def backward_hidden(h, at, value):
                return value * gelu_slope(pre[h, :, at])

            scatters_out = scatter_model(1, h)
            yield from through(h, scatters, gather_hidden(1, h), backward_hidden, U, True, scatters_out)
            norm_grad = yield from finish_model(scatters_out)
            incoming = xn2[h, g.hi, g.lo].astype(F32)
            gradbuf[h] = yield from input_gradient(h, incoming, norm_grad, own_x(h))
            if h == HALVES - 1:
                store_rows(grad_ref, gradbuf)

        def early_chain(h):
            gather = gather_rows("x", 0, h)
            gather.send()
            yield from gather.forward()
            yield
            gather.ready()
            need(2)
            scatters = scatter_hidden(0, h)
            yield from start_hidden(xall.at[0, h], V, True, scatters)
            for c in range(N_CHUNKS):
                yield
                hidden_grad[h, :, unit_slice(c)] = scatters[c].finish()

        def main_chain(h):
            rows, row_numbers = y0_cross(h), stats_cross(h)
            yield from rows.receive()
            yield from row_numbers.receive()
            yield
            rows.ready()
            row_numbers.ready()
            normalize_all(h, xall.at[1, h])
            swapped(h, xn.at[h])
            need(1)
            scatters = scatter_hidden(1, h)
            yield from start_hidden(xn2.at[h], U, False, scatters)
            pick = pick_matrix(d)
            y0_own[h] = jnp.dot(pick.astype(BF16), xall[1, h].reshape(HALF, MODEL), preferred_element_type=F32)
            own_stats[h] = jnp.dot(
                pick, stats[h].reshape(HALF, 128), preferred_element_type=F32, precision=lax.Precision.HIGHEST
            )

            def backward_hidden(h, at, value):
                value = value + up_row[:, at]
                pre[h, :, at] = value
                return hidden_grad[h, :, at] * gelu_slope(value)

            scatters_out = scatter_model(0, h)
            yield from through(h, scatters, gather_hidden(0, h), backward_hidden, U, True, scatters_out)
            norm_grad = yield from finish_model(scatters_out)
            gradbuf[h] = yield from input_gradient(h, own_x(h), norm_grad, y0_own[h])
            send_sem, recv_sem = transposed_sems(h)
            links.send(gradbuf.at[h], xall.at[1, h, g.hi, g.lo], (0, t, d), send_sem, recv_sem)
            links.later(gradbuf.at[h], send_sem, g.pair())

        def late_chain(h):
            gathers = gather_hidden(1, h)
            for c, gather in enumerate(gathers):
                gather.whole[hg.hi, hg.lo] = gelu_value(pre[h, :, unit_slice(c)]).astype(BF16)
                gather.send()
            scatters_out = scatter_model(1, h)
            yield from to_model(h, gathers, V, False, scatters_out)
            mixed = yield from finish_model(scatters_out)
            sendbuf[0, h] = (y0_own[h] + mixed + down_row[...]).astype(BF16)

        if first:
            drive([first_chain(h) for h in range(HALVES)])
        else:
            drive([early_chain(h) for h in range(HALVES)])
            links.finish()
            drive([main_chain(h) for h in range(HALVES)])
            store_rows(grad_ref, gradbuf)
            drive([late_chain(h) for h in range(HALVES)])
            store_rows(out_ref, sendbuf.at[0])
        links.finish()

    for section in range(2):
        pl.when(s == section)(functools.partial(branch, section))
    assert sum(width for _, width in SEM_NAMES.values()) <= SEM_COUNT


def shards(tokens, out_grad, norm_gain, norm_shift, up_weight, up_bias, down_weight, down_bias):
    vmem = pltpu.VMEM
    hidden, model = (2, HALVES, N_CHUNKS), (2, HALVES, M_CHUNKS)
    return pl.pallas_call(
        kernel,
        out_shape=[jax.ShapeDtypeStruct((1, ROWS, MODEL), BF16)] * 2,
        in_specs=[pl.BlockSpec(memory_space=pl.ANY)] * 8,
        out_specs=[pl.BlockSpec(memory_space=vmem)] * 2,
        scratch_shapes=[
            vmem((MODEL, UNITS), BF16),
            vmem((UNITS, MODEL), BF16),
            vmem((1, MODEL), F32),
            vmem((1, MODEL), F32),
            vmem((1, UNITS), F32),
            vmem((1, MODEL), F32),
            vmem((ROWS, MODEL), BF16),
            vmem((2, HALVES, 4, 2, BLOCK, MODEL), BF16),
            vmem((HALVES, 4, 2, BLOCK, MODEL), BF16),
            vmem((HALVES, 4, 2, BLOCK, MODEL), BF16),
            vmem(hidden + (4, 2, BLOCK, N_WIDTH), BF16),
            vmem(hidden + (4, BLOCK, N_WIDTH), BF16),
            vmem(hidden + (4, BLOCK, N_WIDTH), BF16),
            vmem(hidden + (7, BLOCK, N_WIDTH), BF16),
            vmem(hidden + (4, 2, BLOCK, N_WIDTH), BF16),
            vmem((HALVES, HALF, MODEL), F32),
            vmem(model + (4, 2, BLOCK, M_WIDTH), BF16),
            vmem(model + (4, BLOCK, M_WIDTH), BF16),
            vmem(model + (4, BLOCK, M_WIDTH), BF16),
            vmem(model + (7, BLOCK, M_WIDTH), BF16),
            vmem((HALVES, BLOCK, UNITS), F32),
            vmem((HALVES, BLOCK, UNITS), F32),
            vmem((HALVES, 3, 8, BLOCK, 128), F32),
            vmem((HALVES, 4, 2, BLOCK, 128), F32),
            vmem((HALVES, 4, BLOCK, 128), F32),
            vmem((4, HALVES, BLOCK, MODEL), BF16),
            vmem((HALVES, BLOCK, MODEL), BF16),
            vmem((HALVES, BLOCK, MODEL), F32),
            vmem((HALVES, BLOCK, 128), F32),
            pltpu.SemaphoreType.DMA((SEM_COUNT,)),
            pltpu.SemaphoreType.DMA((8,)),
        ],
        compiler_params=pltpu.CompilerParams(
            collective_id=0, has_side_effects=True, vmem_limit_bytes=58 * 2**20
        ),
        cost_estimate=pl.CostEstimate(flops=10**10, bytes_accessed=2 * 10**7, transcendentals=10**5),
        name="relay",
    )(tokens, out_grad, norm_gain, norm_shift, up_weight, up_bias, down_weight, down_bias)


def solution(mesh):
    placed = (
        P("tensor", "dp"),
        P("tensor", "dp"),
        P("section", None),
        P("section", None),
        P("section", "dp", "tensor"),
        P("section", None),
        P("section", "tensor", "dp"),
        P("section", None),
    )
    return jax.shard_map(
        shards,
        mesh=mesh,
        in_specs=placed,
        out_specs=(P("section", "tensor", "dp"), P("section", "tensor", "dp")),
        check_vma=False,
    )
```

```python
import functools

import jax
import jax.numpy as jnp
from jax import lax
from jax.experimental import pallas as pl
from jax.experimental.pallas import tpu as pltpu
from jax.sharding import PartitionSpec as P

D = 12288
ROWS = 32
MODEL = 1536
UNITS = 3072
HALVES = 2
BLOCK = ROWS // HALVES
HALF = 8 * BLOCK
N_CHUNKS, N_WIDTH = 2, 1536
M_CHUNKS, M_WIDTH = 1, 1536
FORWARD_LEAD, MAIN_LEAD, BACKWARD_LEAD = 0, 2, 0
FAR_FIRST = (4, 3, 5, 2, 6, 7, 1)
MESH = pl.DeviceIdType.MESH
F32, BF16 = jnp.float32, jnp.bfloat16

epsilon = 1e-05
root_scale = 0.7978845608028654
cubic_term = 0.044715


def gelu_value(pre_act):
    inner = root_scale * (pre_act + cubic_term * pre_act * pre_act * pre_act)
    return 0.5 * pre_act * (1.0 + jnp.tanh(inner))


def gelu_slope(pre_act):
    inner = root_scale * (pre_act + cubic_term * pre_act * pre_act * pre_act)
    tangent = jnp.tanh(inner)
    return 0.5 * (1.0 + tangent) + 0.5 * pre_act * (1.0 - tangent * tangent) * root_scale * (
        1.0 + 3.0 * cubic_term * pre_act * pre_act
    )


SEM_NAMES = {}


def sem_index(name, count=1):
    if name not in SEM_NAMES:
        SEM_NAMES[name] = sum(width for _, width in SEM_NAMES.values()), count
    return SEM_NAMES[name][0]


SEM_COUNT = 220


class Group:
    def __init__(self, section, axis, d, t):
        self.axis, self.section, self.d, self.t = axis, section, d, t
        self.index = d if axis == "dp" else t
        self.hi, self.lo = self.index // 2, self.index % 2

    def member(self, index):
        if self.axis == "dp":
            return (self.section, index, self.t)
        return (self.section, self.d, index)

    def at(self, hi, lo):
        return self.member(hi * 2 + lo)

    def pair(self):
        return self.at(self.hi, 1 - self.lo)


class Links:
    def __init__(self, sems):
        self.sems = sems
        self.sent = []

    def sem(self, name, offset=0, count=1):
        return self.sems.at[sem_index(name, count) + offset]

    def send(self, src, dst, to, send_sem, recv_sem):
        pltpu.make_async_remote_copy(
            src_ref=src, dst_ref=dst, send_sem=send_sem, recv_sem=recv_sem,
            device_id=to, device_id_type=MESH,
        ).start()

    def wait_recv(self, ref, sem, peer):
        pltpu.make_async_remote_copy(
            src_ref=ref, dst_ref=ref, send_sem=sem, recv_sem=sem,
            device_id=peer, device_id_type=MESH,
        ).wait_recv()

    def later(self, ref, sem, peer):
        self.sent.append((ref, sem, peer))

    def finish(self):
        for ref, sem, peer in self.sent:
            pltpu.make_async_remote_copy(
                src_ref=ref, dst_ref=ref, send_sem=sem, recv_sem=sem,
                device_id=peer, device_id_type=MESH,
            ).wait_send()
        self.sent = []


class PairScatter:
    def __init__(self, links, group, name, part, from_pair, pair_sum, received):
        self.links, self.group, self.name = links, group, name
        self.part, self.from_pair, self.pair_sum = part, from_pair, pair_sum
        self.received = received.at[pl.ds(0, 3)]

    def send(self):
        g, k = self.group, self.links
        src = self.part.at[:, 1 - g.lo]
        sem = k.sem(f"{self.name}/pair_send")
        k.send(src, self.from_pair, g.pair(), sem, k.sem(f"{self.name}/pair_recv"))
        k.later(src, sem, g.pair())

    def middle(self):
        g, k = self.group, self.links
        yield
        k.wait_recv(self.from_pair, k.sem(f"{self.name}/pair_recv"), g.pair())
        total = self.part[:, g.lo].astype(F32) + self.from_pair[...].astype(F32)
        self.pair_sum[...] = total.astype(BF16)
        send_sem = k.sem(f"{self.name}/send")
        for step in (2, 1, 3):
            to = (g.hi + step) % 4
            k.send(self.pair_sum.at[to], self.received.at[step - 1], g.at(to, g.lo), send_sem,
                   k.sem(f"{self.name}/recv"))
        k.later(self.received, send_sem, g.pair())

    def finish(self):
        g, k = self.group, self.links
        k.wait_recv(self.received, k.sem(f"{self.name}/recv"), g.pair())
        total = self.part[g.hi, g.lo].astype(F32) + self.from_pair[g.hi].astype(F32)
        for step in range(3):
            total = total + self.received[step].astype(F32)
        return total


class DirectScatter:
    def __init__(self, links, group, name, part, from_pair, pair_sum, received):
        self.links, self.group, self.name, self.part, self.received = links, group, name, part, received

    def send(self):
        g, k = self.group, self.links
        send_sem = k.sem(f"{self.name}/send")
        for step in FAR_FIRST:
            to = (g.index + step) % 8
            k.send(self.part.at[to // 2, to % 2], self.received.at[step - 1], g.member(to), send_sem,
                   k.sem(f"{self.name}/recv"))
        k.later(self.received, send_sem, g.pair())

    def middle(self):
        return
        yield

    def finish(self):
        g, k = self.group, self.links
        k.wait_recv(self.received, k.sem(f"{self.name}/recv"), g.pair())
        total = self.part[g.hi, g.lo].astype(F32)
        for step in range(7):
            total = total + self.received[step].astype(F32)
        return total


class PairGather:
    def __init__(self, links, group, name, whole, seven):
        self.links, self.group, self.name, self.whole = links, group, name, whole

    def send(self):
        g, k = self.group, self.links
        own = self.whole.at[g.hi, g.lo]
        send_sem = k.sem(f"{self.name}/send")
        for step in (2, 1, 3):
            k.send(own, own, g.at((g.hi + step) % 4, g.lo), send_sem, k.sem(f"{self.name}/recv", step - 1, 3))
        k.send(own, own, g.pair(), send_sem, k.sem(f"{self.name}/pair_recv"))
        k.later(self.whole.at[:, g.lo], send_sem, g.pair())

    def forward(self):
        g, k = self.group, self.links
        send_sem = k.sem(f"{self.name}/on_send")
        yield
        for step in (1, 3, 2):
            block = self.whole.at[(g.hi + 4 - step) % 4, g.lo]
            k.wait_recv(block, k.sem(f"{self.name}/recv", step - 1, 3), g.pair())
            k.send(block, block, g.pair(), send_sem, k.sem(f"{self.name}/pair_recv"))
        k.later(self.whole.at[pl.ds(0, 3), g.lo], send_sem, g.pair())

    def ready(self):
        g, k = self.group, self.links
        k.wait_recv(self.whole.at[:, 1 - g.lo], k.sem(f"{self.name}/pair_recv"), g.pair())


class DirectGather:
    def __init__(self, links, group, name, whole, seven):
        self.links, self.group, self.name, self.whole, self.seven = links, group, name, whole, seven

    def send(self):
        g, k = self.group, self.links
        own = self.whole.at[g.hi, g.lo]
        send_sem = k.sem(f"{self.name}/send")
        for step in FAR_FIRST:
            k.send(own, own, g.member((g.index + step) % 8), send_sem, k.sem(f"{self.name}/recv"))
        k.later(self.seven, send_sem, g.pair())

    def forward(self):
        return
        yield

    def ready(self):
        self.links.wait_recv(self.seven, self.links.sem(f"{self.name}/recv"), self.group.pair())


class Cross:
    def __init__(self, links, group, name, whole, partners):
        self.links, self.group, self.name, self.whole, self.partners = links, group, name, whole, partners

    def send(self, source, four):
        g, k = self.group, self.links
        send_sem = k.sem(f"{self.name}/send")
        for to in self.partners:
            k.send(source, self.whole.at[g.hi, g.lo], to, send_sem, k.sem(f"{self.name}/recv", g.hi, 4))
        k.later(four, send_sem, g.pair())

    def receive(self):
        g, k = self.group, self.links
        send_sem = k.sem(f"{self.name}/on_send")
        yield
        for hi in range(4):
            block = self.whole.at[hi, g.lo]
            k.wait_recv(block, k.sem(f"{self.name}/recv", hi, 4), g.pair())
            k.send(block, block, g.pair(), send_sem, k.sem(f"{self.name}/pair_recv"))
        k.later(self.whole.at[:, g.lo], send_sem, g.pair())

    def ready(self):
        g, k = self.group, self.links
        k.wait_recv(self.whole.at[:, 1 - g.lo], k.sem(f"{self.name}/pair_recv"), g.pair())


def exchange(links, group, name, table, combine):
    send_sem, recv_sem = links.sem(f"{name}/send"), links.sem(f"{name}/recv")
    for step in FAR_FIRST:
        links.send(table.at[0], table.at[step], group.member((group.index + step) % 8), send_sem, recv_sem)
    links.later(table.at[pl.ds(1, 7)], send_sem, group.pair())
    yield
    links.wait_recv(table.at[pl.ds(1, 7)], recv_sem, group.pair())
    return combine([table[k] for k in range(8)])


def pairwise(links, group, name, table, combine):
    pair_send, pair_recv = links.sem(f"{name}/pair_send"), links.sem(f"{name}/pair_recv")
    links.send(table.at[0], table.at[1], group.pair(), pair_send, pair_recv)
    links.later(table.at[0], pair_send, group.pair())
    yield
    links.wait_recv(table.at[1], pair_recv, group.pair())
    table[2] = combine([table[0], table[1]])
    send_sem, recv_sem = links.sem(f"{name}/send"), links.sem(f"{name}/recv")
    for step in (2, 1, 3):
        links.send(table.at[2], table.at[2 + step], group.at((group.hi + step) % 4, group.lo), send_sem, recv_sem)
    links.later(table.at[pl.ds(3, 3)], send_sem, group.pair())
    yield
    links.wait_recv(table.at[pl.ds(3, 3)], recv_sem, group.pair())
    return combine([table[k] for k in range(2, 6)])


def drive(chains, lead=0):
    alive = list(chains)
    if lead:
        for chain in alive:
            next(chain)
    for _ in range(lead):
        next(alive[0])
    while alive:
        for chain in list(alive):
            try:
                next(chain)
            except StopIteration:
                alive.remove(chain)


def add_all(parts):
    return functools.reduce(lambda left, right: left + right, parts)


def join_moments(parts):
    averages = [part[:, 0:1] for part in parts]
    average = add_all(averages) / len(parts)
    squares = add_all([part[:, 64:65] for part in parts])
    spread = add_all([(one - average) * (one - average) for one in averages])
    return two_lanes(average, squares + (MODEL if len(parts) == 2 else 2 * MODEL) * spread)


def two_lanes(first, second):
    lane = lax.broadcasted_iota(jnp.int32, (BLOCK, 128), 1)
    return jnp.where(lane < 64, first, second)


def local_moments(values):
    average = jnp.sum(values, 1, keepdims=True) / MODEL
    centered = values - average
    return two_lanes(average, jnp.sum(centered * centered, 1, keepdims=True))


def row_stats(joined):
    return two_lanes(joined[:, 0:1], lax.rsqrt(joined[:, 64:65] / D + epsilon))


def selection(rows, columns, source):
    row = lax.broadcasted_iota(jnp.int32, (rows, columns), 0)
    column = lax.broadcasted_iota(jnp.int32, (rows, columns), 1)
    return jnp.where(column == source(row), 1.0, 0.0)


WITHIN = BLOCK // 8


def swap_matrix():
    return selection(HALF, HALF, lambda i: ((i // WITHIN) % 8) * BLOCK + (i // BLOCK) * WITHIN + i % WITHIN).astype(BF16)


def pick_matrix(q):
    return selection(BLOCK, HALF, lambda i: (i // WITHIN) * BLOCK + q * WITHIN + i % WITHIN)


def halves_matrix():
    return selection(ROWS, ROWS, lambda i: ((i % BLOCK) // WITHIN) * 4 + (i // BLOCK) * WITHIN + i % WITHIN).astype(BF16)


def whole_matrix():
    return selection(ROWS, ROWS, lambda i: ((i % 4) // WITHIN) * BLOCK + (i // 4) * WITHIN + i % WITHIN).astype(BF16)


def moved(matrix, rows):
    return jnp.dot(matrix, rows, preferred_element_type=F32).astype(BF16)


def transpose_into(target, source):
    rows, columns = source.shape

    @pl.loop(0, rows // 512)
    def _(i):
        at = pl.ds(pl.multiple_of(i * 512, 512), 512)
        for j in range(0, columns, 512):
            target[pl.ds(j, 512), at] = source[at, pl.ds(j, 512)].T


def product(x, w_ref, transposed, k0, depth, n0, width):
    if transposed:
        return lax.dot_general(
            x, w_ref[pl.ds(n0, width), pl.ds(k0, depth)], (((1,), (1,)), ((), ())),
            preferred_element_type=F32,
        )
    return jnp.dot(x, w_ref[pl.ds(k0, depth), pl.ds(n0, width)], preferred_element_type=F32)


def kernel(
    tokens, out_grad, gain, shift, up, up_bias, down, down_bias, out_ref, grad_ref,
    U, V, W, gain_row, shift_row, up_row, down_row, raw, xall, xn, xn2, part, from_pair, pair_sum, received,
    hall, acc, part_m, from_pair_m, pair_sum_m, received_m, pre, hidden_grad, moments, stats, cross_stats,
    sendbuf, gradbuf, y0_own, own_stats, sems, local_sems,
):
    s, d, t = lax.axis_index("section"), lax.axis_index("dp"), lax.axis_index("tensor")

    barrier = pltpu.get_barrier_semaphore()
    greeted = [(s, d + 1 - 2 * (d % 2), t), (1 - s, d, t)]
    greeted += [(s, (d + 2 * k) % 8, t) for k in range(1, 4)]
    greeted += [(s, d, (t + k) % 8) for k in range(1, 8)]
    for to in greeted:
        pl.semaphore_signal(barrier, inc=1, device_id=to, device_id_type=MESH)

    def fetch(src, dst, index):
        copy = pltpu.make_async_copy(src, dst, local_sems.at[index])
        copy.start()
        return copy

    def branch(section):
        first = section == 0
        links = Links(sems)
        hidden_group = Group(section, "dp" if first else "tensor", d, t)
        model_group = Group(section, "tensor" if first else "dp", d, t)
        width_index, unit_index = (d, t) if first else (t, d)
        features = pl.ds(pl.multiple_of(width_index * MODEL, MODEL), MODEL)
        units = pl.ds(pl.multiple_of(unit_index * UNITS, UNITS), UNITS)
        g, hg = model_group, hidden_group
        get_own = fetch(tokens if first else out_grad, raw, 0)
        weights = [(up.at[0], U, 1), (down.at[0], V, 2)]
        gets = {}
        for src, dst, index in weights if first else weights[::-1]:
            gets[index] = fetch(src, dst, index)
        small = [
            fetch(gain.at[:, features], gain_row, 3), fetch(shift.at[:, features], shift_row, 4),
            fetch(up_bias.at[:, units], up_row, 5), fetch(down_bias.at[:, features], down_row, 6),
        ]

        def need(index):
            if index in gets:
                gets.pop(index).wait()

        get_own.wait()
        own_rows = moved(halves_matrix(), raw[...]) if HALVES == 2 else raw[...]
        for h in range(HALVES):
            xall[0, h, g.hi, g.lo] = own_rows[h * BLOCK:(h + 1) * BLOCK]
        for copy in small:
            copy.wait()
        pl.semaphore_wait(barrier, len(greeted))

        def own_x(h):
            return xall[0, h, g.hi, g.lo].astype(F32)

        def scatter_of(group):
            return PairScatter if group.axis == "dp" else DirectScatter

        def gather_of(group):
            return PairGather if group.axis == "dp" else DirectGather

        def scatter_hidden(slot, h):
            return [
                scatter_of(hg)(links, hg, f"h{slot}{h}{c}", part.at[slot, h, c], from_pair.at[slot, h, c],
                               pair_sum.at[slot, h, c], received.at[slot, h, c])
                for c in range(N_CHUNKS)
            ]

        def scatter_model(slot, h):
            return [
                scatter_of(g)(links, g, f"m{slot}{h}{m}", part_m.at[slot, h, m], from_pair_m.at[slot, h, m],
                              pair_sum_m.at[slot, h, m], received_m.at[slot, h, m])
                for m in range(M_CHUNKS)
            ]

        def gather_hidden(slot, h):
            return [gather_of(hg)(links, hg, f"g{slot}{h}{c}", hall.at[slot, h, c], received.at[slot, h, c]) for c in range(N_CHUNKS)]

        def gather_rows(name, slot, h):
            return gather_of(g)(links, g, f"{name}{h}", xall.at[slot, h], received_m.at[slot, h, 0])

        def start_hidden(x_ref, w_ref, transposed, scatters):
            for c, scatter in enumerate(scatters):
                x = x_ref[...].reshape(HALF, MODEL)
                for at in range(0, N_WIDTH, 512):
                    value = product(x, w_ref, transposed, 0, MODEL, c * N_WIDTH + at, 512)
                    scatter.part[:, :, :, pl.ds(at, 512)] = value.astype(BF16).reshape(4, 2, BLOCK, 512)
                scatter.send()
                yield from scatter.middle()

        def to_model(h, gathers, w_ref, transposed, scatters):
            for c, gather in enumerate(gathers):
                yield
                gather.ready()
                x = gather.whole[...].reshape(HALF, N_WIDTH)
                if c < N_CHUNKS - 1:
                    for at in range(0, MODEL, 512):
                        value = product(x, w_ref, transposed, c * N_WIDTH, N_WIDTH, at, 512)
                        acc[h, :, pl.ds(at, 512)] = value if c == 0 else acc[h, :, pl.ds(at, 512)] + value
                    continue
                for m, scatter in enumerate(scatters):
                    for at in range(0, M_WIDTH, 512):
                        value = product(x, w_ref, transposed, c * N_WIDTH, N_WIDTH, m * M_WIDTH + at, 512)
                        if c > 0:
                            value = value + acc[h, :, pl.ds(m * M_WIDTH + at, 512)]
                        scatter.part[:, :, :, pl.ds(at, 512)] = value.astype(BF16).reshape(4, 2, BLOCK, 512)
                    scatter.send()
                    if m >= 1:
                        yield from scatters[m - 1].middle()
            yield from scatters[-1].middle()

        def through(h, scatters, gathers, epilogue, w_ref, transposed, scatters_out):
            for c, scatter in enumerate(scatters):
                yield
                value = epilogue(h, unit_slice(c), scatter.finish())
                gathers[c].whole[hg.hi, hg.lo] = value.astype(BF16)
                gathers[c].send()
                if c >= 1:
                    yield from gathers[c - 1].forward()
            yield from gathers[-1].forward()
            yield from to_model(h, gathers, w_ref, transposed, scatters_out)

        def finish_model(scatters):
            yield
            return jnp.concatenate([scatter.finish() for scatter in scatters], axis=1)

        def normalize_all(h, source):
            for hi in range(4):
                for lo in range(2):
                    average = stats[h, hi, lo][:, 0:1]
                    inverse_dev = stats[h, hi, lo][:, 64:65]
                    unit = (source[hi, lo].astype(F32) - average) * inverse_dev
                    xn[h, hi, lo] = (unit * gain_row[...] + shift_row[...]).astype(BF16)

        def swapped(h, source):
            rows = moved(swap_matrix(), source[...].reshape(HALF, MODEL))
            xn2[h] = rows.reshape(4, 2, BLOCK, MODEL)

        def unit_slice(c):
            return pl.ds(c * N_WIDTH, N_WIDTH)

        def input_gradient(h, incoming, norm_grad, rows):
            average, inverse_dev = own_stats[h][:, 0:1], own_stats[h][:, 64:65]
            unit = (rows - average) * inverse_dev
            scaled = norm_grad * gain_row[...]
            table = moments.at[h, 2]
            table[0] = two_lanes(jnp.sum(scaled, 1, keepdims=True), jnp.sum(scaled * unit, 1, keepdims=True))
            total = yield from (pairwise if first else exchange)(links, hg, f"sums{h}", table, add_all)
            first_mean, second_mean = total[:, 0:1] / D, total[:, 64:65] / D
            return (incoming + inverse_dev * (scaled - first_mean - unit * second_mean)).astype(BF16)

        def store_rows(ref, rows):
            rows = rows[...].reshape(ROWS, MODEL)
            ref[0] = moved(whole_matrix(), rows) if HALVES == 2 else rows

        partners = [(1, 2 * k + t % 2, d) for k in range(4)]

        def y0_cross(h):
            return Cross(links, g, f"y0{h}", xall.at[1, h], partners)

        def stats_sems(h):
            return links.sem(f"y0stats{h}/send"), links.sem(f"y0stats{h}/recv")

        def transposed_sems(h):
            return links.sem(f"g1{h}/send"), links.sem(f"g1{h}/recv")

        def forward_chain(h):
            gather = gather_rows("x", 0, h)
            gather.send()
            moments[h, 0, 0] = local_moments(own_x(h))
            joined = yield from pairwise(links, hg, f"first{h}", moments.at[h, 0], join_moments)
            own_stats[h] = row_stats(joined)
            stats[h, g.hi, g.lo] = own_stats[h]
            stats_gather = DirectGather(links, g, f"st{h}", stats.at[h], moments.at[h, 0, pl.ds(0, 7)])
            stats_gather.send()
            yield
            gather.ready()
            stats_gather.ready()
            normalize_all(h, xall.at[0, h])
            need(1)
            scatters = scatter_hidden(0, h)
            yield from start_hidden(xn.at[h], U, False, scatters)
            need(2)

            def forward_hidden(h, at, value):
                value = value + up_row[:, at]
                pre[h, :, at] = value
                return gelu_value(value)

            scatters_out = scatter_model(0, h)
            yield from through(h, scatters, gather_hidden(0, h), forward_hidden, V, False, scatters_out)
            mixed = yield from finish_model(scatters_out)
            y0 = (own_x(h) + mixed + down_row[...]).astype(BF16)
            sendbuf[0, h] = y0
            y0_cross(h).send(sendbuf.at[0, h], sendbuf.at[pl.ds(0, 4), h])
            moments[h, 1, 0] = local_moments(y0.astype(F32))
            joined = yield from pairwise(links, hg, f"second{h}", moments.at[h, 1], join_moments)
            cross_stats[h, 0] = row_stats(joined)
            send_sem, recv_sem = stats_sems(h)
            for q in range(8):
                links.send(cross_stats.at[h, 0], stats.at[h, g.hi, g.lo], (1, q, d), send_sem, recv_sem)
            links.later(cross_stats.at[h], send_sem, g.pair())

        def backward_chain(h):
            yield
            place = xall.at[1, h, g.hi, g.lo]
            links.wait_recv(place, transposed_sems(h)[1], g.pair())
            gather = gather_rows("g1x", 1, h)
            gather.send()
            yield
            gather.ready()
            swapped(h, xall.at[1, h])
            scatters = scatter_hidden(1, h)
            yield from start_hidden(xn2.at[h], U, False, scatters)

            def backward_hidden(h, at, value):
                return value * gelu_slope(pre[h, :, at])

            scatters_out = scatter_model(1, h)
            yield from through(h, scatters, gather_hidden(1, h), backward_hidden, W, False, scatters_out)
            norm_grad = yield from finish_model(scatters_out)
            incoming = xn2[h, g.hi, g.lo].astype(F32)
            gradbuf[h] = yield from input_gradient(h, incoming, norm_grad, own_x(h))

        def early_chain(h):
            gather = gather_rows("x", 0, h)
            gather.send()
            yield from gather.forward()
            yield
            gather.ready()
            need(2)
            scatters = scatter_hidden(0, h)
            yield from start_hidden(xall.at[0, h], V, True, scatters)
            for c in range(N_CHUNKS):
                yield
                hidden_grad[h, :, unit_slice(c)] = scatters[c].finish()

        def main_chain(h):
            rows = y0_cross(h)
            yield from rows.receive()
            yield
            rows.ready()
            links.wait_recv(stats.at[h], stats_sems(h)[1], g.pair())
            normalize_all(h, xall.at[1, h])
            swapped(h, xn.at[h])
            need(1)
            scatters = scatter_hidden(1, h)
            yield from start_hidden(xn2.at[h], U, False, scatters)
            pick = pick_matrix(d)
            y0_own[h] = jnp.dot(pick.astype(BF16), xall[1, h].reshape(HALF, MODEL), preferred_element_type=F32)
            own_stats[h] = jnp.dot(
                pick, stats[h].reshape(HALF, 128), preferred_element_type=F32, precision=lax.Precision.HIGHEST
            )

            def backward_hidden(h, at, value):
                value = value + up_row[:, at]
                pre[h, :, at] = value
                return hidden_grad[h, :, at] * gelu_slope(value)

            scatters_out = scatter_model(0, h)
            yield from through(h, scatters, gather_hidden(0, h), backward_hidden, W, False, scatters_out)
            norm_grad = yield from finish_model(scatters_out)
            gradbuf[h] = yield from input_gradient(h, own_x(h), norm_grad, y0_own[h])
            send_sem, recv_sem = transposed_sems(h)
            links.send(gradbuf.at[h], xall.at[1, h, g.hi, g.lo], (0, t, d), send_sem, recv_sem)
            links.later(gradbuf.at[h], send_sem, g.pair())

        def late_chain(h):
            gathers = gather_hidden(1, h)
            for c, gather in enumerate(gathers):
                gather.whole[hg.hi, hg.lo] = gelu_value(pre[h, :, unit_slice(c)]).astype(BF16)
                gather.send()
            scatters_out = scatter_model(1, h)
            yield from to_model(h, gathers, V, False, scatters_out)
            mixed = yield from finish_model(scatters_out)
            sendbuf[0, h] = (y0_own[h] + mixed + down_row[...]).astype(BF16)

        if first:
            drive([forward_chain(h) for h in range(HALVES)], FORWARD_LEAD)
            store_rows(out_ref, sendbuf.at[0])
            transpose_into(W, U)
            transpose_into(U, V)
            drive([backward_chain(h) for h in range(HALVES)], BACKWARD_LEAD)
            store_rows(grad_ref, gradbuf)
        else:
            drive([early_chain(h) for h in range(HALVES)])
            links.finish()
            need(1)
            transpose_into(W, U)
            drive([main_chain(h) for h in range(HALVES)], MAIN_LEAD)
            store_rows(grad_ref, gradbuf)
            drive([late_chain(h) for h in range(HALVES)])
            store_rows(out_ref, sendbuf.at[0])
        links.finish()

    for section in range(2):
        pl.when(s == section)(functools.partial(branch, section))
    assert sum(width for _, width in SEM_NAMES.values()) <= SEM_COUNT


def hand_over(out, grad, out_ref, grad_ref):
    out_ref[...] = out[...]
    grad_ref[...] = grad[...]


def shards(tokens, out_grad, norm_gain, norm_shift, up_weight, up_bias, down_weight, down_bias):
    vmem = pltpu.VMEM
    hidden, model = (2, HALVES, N_CHUNKS), (2, HALVES, M_CHUNKS)
    results = pl.pallas_call(
        kernel,
        out_shape=[jax.ShapeDtypeStruct((1, ROWS, MODEL), BF16)] * 2,
        in_specs=[pl.BlockSpec(memory_space=pl.ANY)] * 8,
        out_specs=[pl.BlockSpec(memory_space=vmem)] * 2,
        scratch_shapes=[
            vmem((MODEL, UNITS), BF16),
            vmem((UNITS, MODEL), BF16),
            vmem((UNITS, MODEL), BF16),
            vmem((1, MODEL), F32),
            vmem((1, MODEL), F32),
            vmem((1, UNITS), F32),
            vmem((1, MODEL), F32),
            vmem((ROWS, MODEL), BF16),
            vmem((2, HALVES, 4, 2, BLOCK, MODEL), BF16),
            vmem((HALVES, 4, 2, BLOCK, MODEL), BF16),
            vmem((HALVES, 4, 2, BLOCK, MODEL), BF16),
            vmem(hidden + (4, 2, BLOCK, N_WIDTH), BF16),
            vmem(hidden + (4, BLOCK, N_WIDTH), BF16),
            vmem(hidden + (4, BLOCK, N_WIDTH), BF16),
            vmem(hidden + (7, BLOCK, N_WIDTH), BF16),
            vmem(hidden + (4, 2, BLOCK, N_WIDTH), BF16),
            vmem((HALVES, HALF, MODEL), F32),
            vmem(model + (4, 2, BLOCK, M_WIDTH), BF16),
            vmem(model + (4, BLOCK, M_WIDTH), BF16),
            vmem(model + (4, BLOCK, M_WIDTH), BF16),
            vmem(model + (7, BLOCK, M_WIDTH), BF16),
            vmem((HALVES, BLOCK, UNITS), F32),
            vmem((HALVES, BLOCK, UNITS), F32),
            vmem((HALVES, 3, 8, BLOCK, 128), F32),
            vmem((HALVES, 4, 2, BLOCK, 128), F32),
            vmem((HALVES, 8, BLOCK, 128), F32),
            vmem((4, HALVES, BLOCK, MODEL), BF16),
            vmem((HALVES, BLOCK, MODEL), BF16),
            vmem((HALVES, BLOCK, MODEL), F32),
            vmem((HALVES, BLOCK, 128), F32),
            pltpu.SemaphoreType.DMA((SEM_COUNT,)),
            pltpu.SemaphoreType.DMA((8,)),
        ],
        compiler_params=pltpu.CompilerParams(
            collective_id=0, has_side_effects=True, vmem_limit_bytes=58 * 2**20
        ),
        cost_estimate=pl.CostEstimate(flops=10**10, bytes_accessed=2 * 10**7, transcendentals=10**5),
        name="relay",
    )(tokens, out_grad, norm_gain, norm_shift, up_weight, up_bias, down_weight, down_bias)
    return pl.pallas_call(
        hand_over,
        out_shape=[jax.ShapeDtypeStruct((1, ROWS, MODEL), BF16)] * 2,
        in_specs=[pl.BlockSpec(memory_space=vmem)] * 2,
        out_specs=[pl.BlockSpec(memory_space=vmem)] * 2,
        name="hand_over",
    )(*results)


def solution(mesh):
    placed = (
        P("tensor", "dp"),
        P("tensor", "dp"),
        P("section", None),
        P("section", None),
        P("section", "dp", "tensor"),
        P("section", None),
        P("section", "tensor", "dp"),
        P("section", None),
    )
    return jax.shard_map(
        shards,
        mesh=mesh,
        in_specs=placed,
        out_specs=(P("section", "tensor", "dp"), P("section", "tensor", "dp")),
        check_vma=False,
    )
```

```python
import functools

import jax
import jax.numpy as jnp
from jax import lax
from jax.experimental import pallas as pl
from jax.experimental.pallas import tpu as pltpu
from jax.sharding import PartitionSpec as P

D = 12288
ROWS = 32
MODEL = 1536
UNITS = 3072
HALVES = 2
BLOCK = ROWS // HALVES
HALF = 8 * BLOCK
N_CHUNKS, N_WIDTH = 2, 1536
M_CHUNKS, M_WIDTH = 1, 1536
FORWARD_LEAD, MAIN_LEAD, BACKWARD_LEAD = 0, 1, 0
SEND_ORDER = (1, 7, 3, 5, 4, 2, 6)
MESH = pl.DeviceIdType.MESH
F32, BF16 = jnp.float32, jnp.bfloat16

epsilon = 1e-05
root_scale = 0.7978845608028654
cubic_term = 0.044715


def gelu_value(pre_act):
    inner = root_scale * (pre_act + cubic_term * pre_act * pre_act * pre_act)
    return 0.5 * pre_act * (1.0 + jnp.tanh(inner))


def gelu_slope(pre_act):
    inner = root_scale * (pre_act + cubic_term * pre_act * pre_act * pre_act)
    tangent = jnp.tanh(inner)
    return 0.5 * (1.0 + tangent) + 0.5 * pre_act * (1.0 - tangent * tangent) * root_scale * (
        1.0 + 3.0 * cubic_term * pre_act * pre_act
    )


SEM_NAMES = {}


def sem_index(name, count=1):
    if name not in SEM_NAMES:
        SEM_NAMES[name] = sum(width for _, width in SEM_NAMES.values()), count
    return SEM_NAMES[name][0]


SEM_COUNT = 220


class Group:
    def __init__(self, section, axis, d, t):
        self.axis, self.section, self.d, self.t = axis, section, d, t
        self.index = d if axis == "dp" else t
        self.hi, self.lo = self.index // 2, self.index % 2

    def member(self, index):
        if self.axis == "dp":
            return (self.section, index, self.t)
        return (self.section, self.d, index)

    def at(self, hi, lo):
        return self.member(hi * 2 + lo)

    def pair(self):
        return self.at(self.hi, 1 - self.lo)


class Links:
    def __init__(self, sems):
        self.sems = sems
        self.sent = []

    def sem(self, name, offset=0, count=1):
        return self.sems.at[sem_index(name, count) + offset]

    def send(self, src, dst, to, send_sem, recv_sem):
        pltpu.make_async_remote_copy(
            src_ref=src, dst_ref=dst, send_sem=send_sem, recv_sem=recv_sem,
            device_id=to, device_id_type=MESH,
        ).start()

    def wait_recv(self, ref, sem, peer):
        pltpu.make_async_remote_copy(
            src_ref=ref, dst_ref=ref, send_sem=sem, recv_sem=sem,
            device_id=peer, device_id_type=MESH,
        ).wait_recv()

    def later(self, ref, sem, peer):
        self.sent.append((ref, sem, peer))

    def finish(self):
        for ref, sem, peer in self.sent:
            pltpu.make_async_remote_copy(
                src_ref=ref, dst_ref=ref, send_sem=sem, recv_sem=sem,
                device_id=peer, device_id_type=MESH,
            ).wait_send()
        self.sent = []


class PairScatter:
    def __init__(self, links, group, name, part, from_pair, pair_sum, received):
        self.links, self.group, self.name = links, group, name
        self.part, self.from_pair, self.pair_sum = part, from_pair, pair_sum
        self.received = received.at[pl.ds(0, 3)]

    def send(self):
        g, k = self.group, self.links
        src = self.part.at[:, 1 - g.lo]
        sem = k.sem(f"{self.name}/pair_send")
        k.send(src, self.from_pair, g.pair(), sem, k.sem(f"{self.name}/pair_recv"))
        k.later(src, sem, g.pair())

    def middle(self):
        g, k = self.group, self.links
        yield
        k.wait_recv(self.from_pair, k.sem(f"{self.name}/pair_recv"), g.pair())
        total = self.part[:, g.lo].astype(F32) + self.from_pair[...].astype(F32)
        self.pair_sum[...] = total.astype(BF16)
        send_sem = k.sem(f"{self.name}/send")
        for step in (2, 1, 3):
            to = (g.hi + step) % 4
            k.send(self.pair_sum.at[to], self.received.at[step - 1], g.at(to, g.lo), send_sem,
                   k.sem(f"{self.name}/recv"))
        k.later(self.received, send_sem, g.pair())

    def finish(self):
        g, k = self.group, self.links
        k.wait_recv(self.received, k.sem(f"{self.name}/recv"), g.pair())
        total = self.part[g.hi, g.lo].astype(F32) + self.from_pair[g.hi].astype(F32)
        for step in range(3):
            total = total + self.received[step].astype(F32)
        return total


class DirectScatter:
    def __init__(self, links, group, name, part, from_pair, pair_sum, received):
        self.links, self.group, self.name, self.part, self.received = links, group, name, part, received

    def send(self):
        g, k = self.group, self.links
        send_sem = k.sem(f"{self.name}/send")
        for step in SEND_ORDER:
            to = (g.index + step) % 8
            k.send(self.part.at[to // 2, to % 2], self.received.at[step - 1], g.member(to), send_sem,
                   k.sem(f"{self.name}/recv"))
        k.later(self.received, send_sem, g.pair())

    def middle(self):
        return
        yield

    def finish(self):
        g, k = self.group, self.links
        k.wait_recv(self.received, k.sem(f"{self.name}/recv"), g.pair())
        total = self.part[g.hi, g.lo].astype(F32)
        for step in range(7):
            total = total + self.received[step].astype(F32)
        return total


class PairGather:
    def __init__(self, links, group, name, whole, seven):
        self.links, self.group, self.name, self.whole = links, group, name, whole

    def send(self):
        g, k = self.group, self.links
        own = self.whole.at[g.hi, g.lo]
        send_sem = k.sem(f"{self.name}/send")
        for step in (2, 1, 3):
            k.send(own, own, g.at((g.hi + step) % 4, g.lo), send_sem, k.sem(f"{self.name}/recv", step - 1, 3))
        k.send(own, own, g.pair(), send_sem, k.sem(f"{self.name}/pair_recv"))
        k.later(self.whole.at[:, g.lo], send_sem, g.pair())

    def forward(self):
        g, k = self.group, self.links
        send_sem = k.sem(f"{self.name}/on_send")
        yield
        for step in (1, 3, 2):
            block = self.whole.at[(g.hi + 4 - step) % 4, g.lo]
            k.wait_recv(block, k.sem(f"{self.name}/recv", step - 1, 3), g.pair())
            k.send(block, block, g.pair(), send_sem, k.sem(f"{self.name}/pair_recv"))
        k.later(self.whole.at[pl.ds(0, 3), g.lo], send_sem, g.pair())

    def ready(self):
        g, k = self.group, self.links
        k.wait_recv(self.whole.at[:, 1 - g.lo], k.sem(f"{self.name}/pair_recv"), g.pair())


class DirectGather:
    def __init__(self, links, group, name, whole, seven):
        self.links, self.group, self.name, self.whole, self.seven = links, group, name, whole, seven

    def send(self):
        g, k = self.group, self.links
        own = self.whole.at[g.hi, g.lo]
        send_sem = k.sem(f"{self.name}/send")
        for step in SEND_ORDER:
            k.send(own, own, g.member((g.index + step) % 8), send_sem, k.sem(f"{self.name}/recv"))
        k.later(self.seven, send_sem, g.pair())

    def forward(self):
        return
        yield

    def ready(self):
        self.links.wait_recv(self.seven, self.links.sem(f"{self.name}/recv"), self.group.pair())


class Cross:
    def __init__(self, links, group, name, whole, partners):
        self.links, self.group, self.name, self.whole, self.partners = links, group, name, whole, partners

    def send(self, source, four):
        g, k = self.group, self.links
        send_sem = k.sem(f"{self.name}/send")
        for to in self.partners:
            k.send(source, self.whole.at[g.hi, g.lo], to, send_sem, k.sem(f"{self.name}/recv", g.hi, 4))
        k.later(four, send_sem, g.pair())

    def receive(self):
        g, k = self.group, self.links
        send_sem = k.sem(f"{self.name}/on_send")
        yield
        for hi in range(4):
            block = self.whole.at[hi, g.lo]
            k.wait_recv(block, k.sem(f"{self.name}/recv", hi, 4), g.pair())
            k.send(block, block, g.pair(), send_sem, k.sem(f"{self.name}/pair_recv"))
        k.later(self.whole.at[:, g.lo], send_sem, g.pair())

    def ready(self):
        g, k = self.group, self.links
        k.wait_recv(self.whole.at[:, 1 - g.lo], k.sem(f"{self.name}/pair_recv"), g.pair())


def exchange(links, group, name, table, combine):
    send_sem, recv_sem = links.sem(f"{name}/send"), links.sem(f"{name}/recv")
    for step in SEND_ORDER:
        links.send(table.at[0], table.at[step], group.member((group.index + step) % 8), send_sem, recv_sem)
    links.later(table.at[pl.ds(1, 7)], send_sem, group.pair())
    yield
    links.wait_recv(table.at[pl.ds(1, 7)], recv_sem, group.pair())
    return combine([table[k] for k in range(8)])


def pairwise(links, group, name, table, combine):
    pair_send, pair_recv = links.sem(f"{name}/pair_send"), links.sem(f"{name}/pair_recv")
    links.send(table.at[0], table.at[1], group.pair(), pair_send, pair_recv)
    links.later(table.at[0], pair_send, group.pair())
    yield
    links.wait_recv(table.at[1], pair_recv, group.pair())
    table[2] = combine([table[0], table[1]])
    send_sem, recv_sem = links.sem(f"{name}/send"), links.sem(f"{name}/recv")
    for step in (2, 1, 3):
        links.send(table.at[2], table.at[2 + step], group.at((group.hi + step) % 4, group.lo), send_sem, recv_sem)
    links.later(table.at[pl.ds(3, 3)], send_sem, group.pair())
    yield
    links.wait_recv(table.at[pl.ds(3, 3)], recv_sem, group.pair())
    return combine([table[k] for k in range(2, 6)])


def drive(chains, lead=0):
    alive = list(chains)
    if lead:
        for chain in alive:
            next(chain)
    for _ in range(lead):
        next(alive[0])
    while alive:
        for chain in list(alive):
            try:
                next(chain)
            except StopIteration:
                alive.remove(chain)


def add_all(parts):
    return functools.reduce(lambda left, right: left + right, parts)


def join_moments(parts):
    averages = [part[:, 0:1] for part in parts]
    average = add_all(averages) / len(parts)
    squares = add_all([part[:, 64:65] for part in parts])
    spread = add_all([(one - average) * (one - average) for one in averages])
    return two_lanes(average, squares + (MODEL if len(parts) == 2 else 2 * MODEL) * spread)


def two_lanes(first, second):
    lane = lax.broadcasted_iota(jnp.int32, (BLOCK, 128), 1)
    return jnp.where(lane < 64, first, second)


def local_moments(values):
    average = jnp.sum(values, 1, keepdims=True) / MODEL
    centered = values - average
    return two_lanes(average, jnp.sum(centered * centered, 1, keepdims=True))


def row_stats(joined):
    return two_lanes(joined[:, 0:1], lax.rsqrt(joined[:, 64:65] / D + epsilon))


def selection(rows, columns, source):
    row = lax.broadcasted_iota(jnp.int32, (rows, columns), 0)
    column = lax.broadcasted_iota(jnp.int32, (rows, columns), 1)
    return jnp.where(column == source(row), 1.0, 0.0)


WITHIN = BLOCK // 8


def swap_matrix():
    return selection(HALF, HALF, lambda i: ((i // WITHIN) % 8) * BLOCK + (i // BLOCK) * WITHIN + i % WITHIN).astype(BF16)


def pick_matrix(q):
    return selection(BLOCK, HALF, lambda i: (i // WITHIN) * BLOCK + q * WITHIN + i % WITHIN)


def halves_matrix():
    return selection(ROWS, ROWS, lambda i: ((i % BLOCK) // WITHIN) * 4 + (i // BLOCK) * WITHIN + i % WITHIN).astype(BF16)


def whole_matrix():
    return selection(ROWS, ROWS, lambda i: ((i % 4) // WITHIN) * BLOCK + (i // 4) * WITHIN + i % WITHIN).astype(BF16)


def moved(matrix, rows):
    return jnp.dot(matrix, rows, preferred_element_type=F32).astype(BF16)


def transpose_into(target, source):
    rows, columns = source.shape

    @pl.loop(0, rows // 512)
    def _(i):
        at = pl.ds(pl.multiple_of(i * 512, 512), 512)
        for j in range(0, columns, 512):
            target[pl.ds(j, 512), at] = source[at, pl.ds(j, 512)].T


def product(x, w_ref, transposed, k0, depth, n0, width):
    if transposed:
        return lax.dot_general(
            x, w_ref[pl.ds(n0, width), pl.ds(k0, depth)], (((1,), (1,)), ((), ())),
            preferred_element_type=F32,
        )
    return jnp.dot(x, w_ref[pl.ds(k0, depth), pl.ds(n0, width)], preferred_element_type=F32)


def kernel(
    tokens, out_grad, gain, shift, up, up_bias, down, down_bias, out_ref, grad_ref,
    U, V, W, gain_row, shift_row, up_row, down_row, raw, xall, xn, xn2, part, from_pair, pair_sum, received,
    hall, acc, part_m, from_pair_m, pair_sum_m, received_m, pre, hidden_grad, moments, stats, cross_stats,
    sendbuf, gradbuf, y0_own, own_stats, sems, local_sems,
):
    s, d, t = lax.axis_index("section"), lax.axis_index("dp"), lax.axis_index("tensor")

    barrier = pltpu.get_barrier_semaphore()
    greeted = [(s, d + 1 - 2 * (d % 2), t), (1 - s, d, t)]
    greeted += [(s, (d + 2 * k) % 8, t) for k in range(1, 4)]
    greeted += [(s, d, (t + k) % 8) for k in range(1, 8)]
    for to in greeted:
        pl.semaphore_signal(barrier, inc=1, device_id=to, device_id_type=MESH)

    def fetch(src, dst, index):
        copy = pltpu.make_async_copy(src, dst, local_sems.at[index])
        copy.start()
        return copy

    def branch(section):
        first = section == 0
        links = Links(sems)
        hidden_group = Group(section, "dp" if first else "tensor", d, t)
        model_group = Group(section, "tensor" if first else "dp", d, t)
        width_index, unit_index = (d, t) if first else (t, d)
        features = pl.ds(pl.multiple_of(width_index * MODEL, MODEL), MODEL)
        units = pl.ds(pl.multiple_of(unit_index * UNITS, UNITS), UNITS)
        g, hg = model_group, hidden_group
        get_own = fetch(tokens if first else out_grad, raw, 0)
        weights = [(up.at[0], U, 1), (down.at[0], V, 2)]
        gets = {}
        for src, dst, index in weights if first else weights[::-1]:
            gets[index] = fetch(src, dst, index)
        small = [
            fetch(gain.at[:, features], gain_row, 3), fetch(shift.at[:, features], shift_row, 4),
            fetch(up_bias.at[:, units], up_row, 5), fetch(down_bias.at[:, features], down_row, 6),
        ]

        def need(index):
            if index in gets:
                gets.pop(index).wait()

        get_own.wait()
        own_rows = moved(halves_matrix(), raw[...]) if HALVES == 2 else raw[...]
        for h in range(HALVES):
            xall[0, h, g.hi, g.lo] = own_rows[h * BLOCK:(h + 1) * BLOCK]
        def own_x(h):
            return xall[0, h, g.hi, g.lo].astype(F32)

        if first:
            for h in range(HALVES):
                moments[h, 0, 0] = local_moments(own_x(h))
        for copy in small:
            copy.wait()
        pl.semaphore_wait(barrier, len(greeted))

        def scatter_of(group):
            return PairScatter if group.axis == "dp" else DirectScatter

        def gather_of(group):
            return PairGather if group.axis == "dp" else DirectGather

        def scatter_hidden(slot, h):
            return [
                scatter_of(hg)(links, hg, f"h{slot}{h}{c}", part.at[slot, h, c], from_pair.at[slot, h, c],
                               pair_sum.at[slot, h, c], received.at[slot, h, c])
                for c in range(N_CHUNKS)
            ]

        def scatter_model(slot, h):
            return [
                scatter_of(g)(links, g, f"m{slot}{h}{m}", part_m.at[slot, h, m], from_pair_m.at[slot, h, m],
                              pair_sum_m.at[slot, h, m], received_m.at[slot, h, m])
                for m in range(M_CHUNKS)
            ]

        def gather_hidden(slot, h):
            return [gather_of(hg)(links, hg, f"g{slot}{h}{c}", hall.at[slot, h, c], received.at[slot, h, c]) for c in range(N_CHUNKS)]

        def gather_rows(name, slot, h):
            return gather_of(g)(links, g, f"{name}{h}", xall.at[slot, h], received_m.at[slot, h, 0])

        def start_hidden(x_ref, w_ref, transposed, scatters):
            for c, scatter in enumerate(scatters):
                x = x_ref[...].reshape(HALF, MODEL)
                for at in range(0, N_WIDTH, 512):
                    value = product(x, w_ref, transposed, 0, MODEL, c * N_WIDTH + at, 512)
                    scatter.part[:, :, :, pl.ds(at, 512)] = value.astype(BF16).reshape(4, 2, BLOCK, 512)
                scatter.send()
                yield from scatter.middle()

        def to_model(h, gathers, w_ref, transposed, scatters):
            for c, gather in enumerate(gathers):
                yield
                gather.ready()
                x = gather.whole[...].reshape(HALF, N_WIDTH)
                if c < N_CHUNKS - 1:
                    for at in range(0, MODEL, 512):
                        value = product(x, w_ref, transposed, c * N_WIDTH, N_WIDTH, at, 512)
                        acc[h, :, pl.ds(at, 512)] = value if c == 0 else acc[h, :, pl.ds(at, 512)] + value
                    continue
                for m, scatter in enumerate(scatters):
                    for at in range(0, M_WIDTH, 512):
                        value = product(x, w_ref, transposed, c * N_WIDTH, N_WIDTH, m * M_WIDTH + at, 512)
                        if c > 0:
                            value = value + acc[h, :, pl.ds(m * M_WIDTH + at, 512)]
                        scatter.part[:, :, :, pl.ds(at, 512)] = value.astype(BF16).reshape(4, 2, BLOCK, 512)
                    scatter.send()
                    if m >= 1:
                        yield from scatters[m - 1].middle()
            yield from scatters[-1].middle()

        def through(h, scatters, gathers, epilogue, w_ref, transposed, scatters_out):
            for c, scatter in enumerate(scatters):
                yield
                value = epilogue(h, unit_slice(c), scatter.finish())
                gathers[c].whole[hg.hi, hg.lo] = value.astype(BF16)
                gathers[c].send()
                if c >= 1:
                    yield from gathers[c - 1].forward()
            yield from gathers[-1].forward()
            yield from to_model(h, gathers, w_ref, transposed, scatters_out)

        def finish_model(scatters):
            yield
            return jnp.concatenate([scatter.finish() for scatter in scatters], axis=1)

        def normalize_all(h, source):
            for hi in range(4):
                for lo in range(2):
                    average = stats[h, hi, lo][:, 0:1]
                    inverse_dev = stats[h, hi, lo][:, 64:65]
                    unit = (source[hi, lo].astype(F32) - average) * inverse_dev
                    xn[h, hi, lo] = (unit * gain_row[...] + shift_row[...]).astype(BF16)

        def swapped(h, source):
            rows = moved(swap_matrix(), source[...].reshape(HALF, MODEL))
            xn2[h] = rows.reshape(4, 2, BLOCK, MODEL)

        def unit_slice(c):
            return pl.ds(c * N_WIDTH, N_WIDTH)

        def input_gradient(h, incoming, norm_grad, rows):
            average, inverse_dev = own_stats[h][:, 0:1], own_stats[h][:, 64:65]
            unit = (rows - average) * inverse_dev
            scaled = norm_grad * gain_row[...]
            table = moments.at[h, 2]
            table[0] = two_lanes(jnp.sum(scaled, 1, keepdims=True), jnp.sum(scaled * unit, 1, keepdims=True))
            total = yield from (pairwise if first else exchange)(links, hg, f"sums{h}", table, add_all)
            first_mean, second_mean = total[:, 0:1] / D, total[:, 64:65] / D
            return (incoming + inverse_dev * (scaled - first_mean - unit * second_mean)).astype(BF16)

        def store_rows(ref, rows):
            rows = rows[...].reshape(ROWS, MODEL)
            ref[0] = moved(whole_matrix(), rows) if HALVES == 2 else rows

        partners = [(1, 2 * k + t % 2, d) for k in range(4)]

        def y0_cross(h):
            return Cross(links, g, f"y0{h}", xall.at[1, h], partners)

        def stats_sems(h):
            return links.sem(f"y0stats{h}/send"), links.sem(f"y0stats{h}/recv")

        def transposed_sems(h):
            return links.sem(f"g1{h}/send"), links.sem(f"g1{h}/recv")

        def forward_chain(h):
            gather = gather_rows("x", 0, h)
            gather.send()
            joined = yield from pairwise(links, hg, f"first{h}", moments.at[h, 0], join_moments)
            own_stats[h] = row_stats(joined)
            stats[h, g.hi, g.lo] = own_stats[h]
            stats_gather = DirectGather(links, g, f"st{h}", stats.at[h], moments.at[h, 0, pl.ds(0, 7)])
            stats_gather.send()
            yield
            gather.ready()
            stats_gather.ready()
            normalize_all(h, xall.at[0, h])
            need(1)
            scatters = scatter_hidden(0, h)
            yield from start_hidden(xn.at[h], U, False, scatters)
            need(2)

            def forward_hidden(h, at, value):
                value = value + up_row[:, at]
                pre[h, :, at] = value
                return gelu_value(value)

            scatters_out = scatter_model(0, h)
            yield from through(h, scatters, gather_hidden(0, h), forward_hidden, V, False, scatters_out)
            mixed = yield from finish_model(scatters_out)
            y0 = (own_x(h) + mixed + down_row[...]).astype(BF16)
            sendbuf[0, h] = y0
            y0_cross(h).send(sendbuf.at[0, h], sendbuf.at[pl.ds(0, 4), h])
            moments[h, 1, 0] = local_moments(y0.astype(F32))
            joined = yield from pairwise(links, hg, f"second{h}", moments.at[h, 1], join_moments)
            cross_stats[h, 0] = row_stats(joined)
            send_sem, recv_sem = stats_sems(h)
            for q in range(8):
                links.send(cross_stats.at[h, 0], stats.at[h, g.hi, g.lo], (1, q, d), send_sem, recv_sem)
            links.later(cross_stats.at[h], send_sem, g.pair())

        def backward_chain(h):
            yield
            place = xall.at[1, h, g.hi, g.lo]
            links.wait_recv(place, transposed_sems(h)[1], g.pair())
            gather = gather_rows("g1x", 1, h)
            gather.send()
            yield
            gather.ready()
            swapped(h, xall.at[1, h])
            scatters = scatter_hidden(1, h)
            yield from start_hidden(xn2.at[h], U, False, scatters)

            def backward_hidden(h, at, value):
                return value * gelu_slope(pre[h, :, at])

            scatters_out = scatter_model(1, h)
            yield from through(h, scatters, gather_hidden(1, h), backward_hidden, W, False, scatters_out)
            norm_grad = yield from finish_model(scatters_out)
            incoming = xn2[h, g.hi, g.lo].astype(F32)
            gradbuf[h] = yield from input_gradient(h, incoming, norm_grad, own_x(h))

        def early_chain(h):
            gather = gather_rows("x", 0, h)
            gather.send()
            yield from gather.forward()
            yield
            gather.ready()
            need(2)
            scatters = scatter_hidden(0, h)
            yield from start_hidden(xall.at[0, h], V, True, scatters)
            for c in range(N_CHUNKS):
                yield
                hidden_grad[h, :, unit_slice(c)] = scatters[c].finish()

        def main_chain(h):
            rows = y0_cross(h)
            yield from rows.receive()
            yield
            rows.ready()
            links.wait_recv(stats.at[h], stats_sems(h)[1], g.pair())
            normalize_all(h, xall.at[1, h])
            swapped(h, xn.at[h])
            need(1)
            scatters = scatter_hidden(1, h)
            yield from start_hidden(xn2.at[h], U, False, scatters)
            pick = pick_matrix(d)
            y0_own[h] = jnp.dot(pick.astype(BF16), xall[1, h].reshape(HALF, MODEL), preferred_element_type=F32)
            own_stats[h] = jnp.dot(
                pick, stats[h].reshape(HALF, 128), preferred_element_type=F32, precision=lax.Precision.HIGHEST
            )

            def backward_hidden(h, at, value):
                value = value + up_row[:, at]
                pre[h, :, at] = value
                return hidden_grad[h, :, at] * gelu_slope(value)

            scatters_out = scatter_model(0, h)
            yield from through(h, scatters, gather_hidden(0, h), backward_hidden, W, False, scatters_out)
            norm_grad = yield from finish_model(scatters_out)
            gradbuf[h] = yield from input_gradient(h, own_x(h), norm_grad, y0_own[h])
            send_sem, recv_sem = transposed_sems(h)
            links.send(gradbuf.at[h], xall.at[1, h, g.hi, g.lo], (0, t, d), send_sem, recv_sem)
            links.later(gradbuf.at[h], send_sem, g.pair())

        def late_chain(h):
            gathers = gather_hidden(1, h)
            for c, gather in enumerate(gathers):
                gather.whole[hg.hi, hg.lo] = gelu_value(pre[h, :, unit_slice(c)]).astype(BF16)
                gather.send()
            scatters_out = scatter_model(1, h)
            yield from to_model(h, gathers, V, False, scatters_out)
            mixed = yield from finish_model(scatters_out)
            sendbuf[0, h] = (y0_own[h] + mixed + down_row[...]).astype(BF16)

        if first:
            drive([forward_chain(h) for h in range(HALVES)], FORWARD_LEAD)
            store_rows(out_ref, sendbuf.at[0])
            transpose_into(W, U)
            transpose_into(U, V)
            links.finish()
            drive([backward_chain(h) for h in range(HALVES)], BACKWARD_LEAD)
            store_rows(grad_ref, gradbuf)
        else:
            drive([early_chain(h) for h in range(HALVES)])
            links.finish()
            need(1)
            transpose_into(W, U)
            drive([main_chain(h) for h in range(HALVES)], MAIN_LEAD)
            store_rows(grad_ref, gradbuf)
            drive([late_chain(h) for h in range(HALVES)])
            store_rows(out_ref, sendbuf.at[0])
        links.finish()

    for section in range(2):
        pl.when(s == section)(functools.partial(branch, section))
    assert sum(width for _, width in SEM_NAMES.values()) <= SEM_COUNT


def hand_over(out, grad, out_ref, grad_ref):
    out_ref[...] = out[...]
    grad_ref[...] = grad[...]


def shards(tokens, out_grad, norm_gain, norm_shift, up_weight, up_bias, down_weight, down_bias):
    vmem = pltpu.VMEM
    hidden, model = (2, HALVES, N_CHUNKS), (2, HALVES, M_CHUNKS)
    results = pl.pallas_call(
        kernel,
        out_shape=[jax.ShapeDtypeStruct((1, ROWS, MODEL), BF16)] * 2,
        in_specs=[pl.BlockSpec(memory_space=pl.ANY)] * 8,
        out_specs=[pl.BlockSpec(memory_space=vmem)] * 2,
        scratch_shapes=[
            vmem((MODEL, UNITS), BF16),
            vmem((UNITS, MODEL), BF16),
            vmem((UNITS, MODEL), BF16),
            vmem((1, MODEL), F32),
            vmem((1, MODEL), F32),
            vmem((1, UNITS), F32),
            vmem((1, MODEL), F32),
            vmem((ROWS, MODEL), BF16),
            vmem((2, HALVES, 4, 2, BLOCK, MODEL), BF16),
            vmem((HALVES, 4, 2, BLOCK, MODEL), BF16),
            vmem((HALVES, 4, 2, BLOCK, MODEL), BF16),
            vmem(hidden + (4, 2, BLOCK, N_WIDTH), BF16),
            vmem(hidden + (4, BLOCK, N_WIDTH), BF16),
            vmem(hidden + (4, BLOCK, N_WIDTH), BF16),
            vmem(hidden + (7, BLOCK, N_WIDTH), BF16),
            vmem(hidden + (4, 2, BLOCK, N_WIDTH), BF16),
            vmem((HALVES, HALF, MODEL), F32),
            vmem(model + (4, 2, BLOCK, M_WIDTH), BF16),
            vmem(model + (4, BLOCK, M_WIDTH), BF16),
            vmem(model + (4, BLOCK, M_WIDTH), BF16),
            vmem(model + (7, BLOCK, M_WIDTH), BF16),
            vmem((HALVES, BLOCK, UNITS), F32),
            vmem((HALVES, BLOCK, UNITS), F32),
            vmem((HALVES, 3, 8, BLOCK, 128), F32),
            vmem((HALVES, 4, 2, BLOCK, 128), F32),
            vmem((HALVES, 8, BLOCK, 128), F32),
            vmem((4, HALVES, BLOCK, MODEL), BF16),
            vmem((HALVES, BLOCK, MODEL), BF16),
            vmem((HALVES, BLOCK, MODEL), F32),
            vmem((HALVES, BLOCK, 128), F32),
            pltpu.SemaphoreType.DMA((SEM_COUNT,)),
            pltpu.SemaphoreType.DMA((8,)),
        ],
        compiler_params=pltpu.CompilerParams(
            collective_id=0, has_side_effects=True, vmem_limit_bytes=58 * 2**20
        ),
        cost_estimate=pl.CostEstimate(flops=10**10, bytes_accessed=2 * 10**7, transcendentals=10**5),
        name="relay",
    )(tokens, out_grad, norm_gain, norm_shift, up_weight, up_bias, down_weight, down_bias)
    return pl.pallas_call(
        hand_over,
        out_shape=[jax.ShapeDtypeStruct((1, ROWS, MODEL), BF16)] * 2,
        in_specs=[pl.BlockSpec(memory_space=vmem)] * 2,
        out_specs=[pl.BlockSpec(memory_space=vmem)] * 2,
        name="hand_over",
    )(*results)


def solution(mesh):
    placed = (
        P("tensor", "dp"),
        P("tensor", "dp"),
        P("section", None),
        P("section", None),
        P("section", "dp", "tensor"),
        P("section", None),
        P("section", "tensor", "dp"),
        P("section", None),
    )
    return jax.shard_map(
        shards,
        mesh=mesh,
        in_specs=placed,
        out_specs=(P("section", "tensor", "dp"), P("section", "tensor", "dp")),
        check_vma=False,
    )
```

```python
import functools

import jax
import jax.numpy as jnp
from jax import lax
from jax.experimental import pallas as pl
from jax.experimental.pallas import tpu as pltpu
from jax.sharding import PartitionSpec as P

D = 12288
ROWS = 32
MODEL = 1536
UNITS = 3072
HALVES = 2
BLOCK = ROWS // HALVES
HALF = 8 * BLOCK
N_CHUNKS, N_WIDTH = 2, 1536
M_CHUNKS, M_WIDTH = 1, 1536
FORWARD_LEAD, MAIN_LEAD, BACKWARD_LEAD = 0, 1, 0
SEND_ORDER = (1, 7, 3, 5, 4, 2, 6)
MESH = pl.DeviceIdType.MESH
F32, BF16 = jnp.float32, jnp.bfloat16

epsilon = 1e-05
root_scale = 0.7978845608028654
cubic_term = 0.044715


def gelu_value(pre_act):
    inner = root_scale * (pre_act + cubic_term * pre_act * pre_act * pre_act)
    return 0.5 * pre_act * (1.0 + jnp.tanh(inner))


def gelu_slope(pre_act):
    inner = root_scale * (pre_act + cubic_term * pre_act * pre_act * pre_act)
    tangent = jnp.tanh(inner)
    return 0.5 * (1.0 + tangent) + 0.5 * pre_act * (1.0 - tangent * tangent) * root_scale * (
        1.0 + 3.0 * cubic_term * pre_act * pre_act
    )


SEM_NAMES = {}


def sem_index(name, count=1):
    if name not in SEM_NAMES:
        SEM_NAMES[name] = sum(width for _, width in SEM_NAMES.values()), count
    return SEM_NAMES[name][0]


SEM_COUNT = 220


class Group:
    def __init__(self, section, axis, d, t):
        self.axis, self.section, self.d, self.t = axis, section, d, t
        self.index = d if axis == "dp" else t
        self.hi, self.lo = self.index // 2, self.index % 2

    def member(self, index):
        if self.axis == "dp":
            return (self.section, index, self.t)
        return (self.section, self.d, index)

    def at(self, hi, lo):
        return self.member(hi * 2 + lo)

    def pair(self):
        return self.at(self.hi, 1 - self.lo)


class Links:
    def __init__(self, sems):
        self.sems = sems
        self.sent = []

    def sem(self, name, offset=0, count=1):
        return self.sems.at[sem_index(name, count) + offset]

    def send(self, src, dst, to, send_sem, recv_sem):
        pltpu.make_async_remote_copy(
            src_ref=src, dst_ref=dst, send_sem=send_sem, recv_sem=recv_sem,
            device_id=to, device_id_type=MESH,
        ).start()

    def wait_recv(self, ref, sem, peer):
        pltpu.make_async_remote_copy(
            src_ref=ref, dst_ref=ref, send_sem=sem, recv_sem=sem,
            device_id=peer, device_id_type=MESH,
        ).wait_recv()

    def later(self, ref, sem, peer):
        self.sent.append((ref, sem, peer))

    def finish(self):
        for ref, sem, peer in self.sent:
            pltpu.make_async_remote_copy(
                src_ref=ref, dst_ref=ref, send_sem=sem, recv_sem=sem,
                device_id=peer, device_id_type=MESH,
            ).wait_send()
        self.sent = []


class PairScatter:
    def __init__(self, links, group, name, part, from_pair, pair_sum, received):
        self.links, self.group, self.name = links, group, name
        self.part, self.from_pair, self.pair_sum = part, from_pair, pair_sum
        self.received = received.at[pl.ds(0, 3)]

    def send(self):
        g, k = self.group, self.links
        src = self.part.at[:, 1 - g.lo]
        sem = k.sem(f"{self.name}/pair_send")
        k.send(src, self.from_pair, g.pair(), sem, k.sem(f"{self.name}/pair_recv"))
        k.later(src, sem, g.pair())

    def middle(self):
        g, k = self.group, self.links
        yield
        k.wait_recv(self.from_pair, k.sem(f"{self.name}/pair_recv"), g.pair())
        total = self.part[:, g.lo].astype(F32) + self.from_pair[...].astype(F32)
        self.pair_sum[...] = total.astype(BF16)
        send_sem = k.sem(f"{self.name}/send")
        for step in (2, 1, 3):
            to = (g.hi + step) % 4
            k.send(self.pair_sum.at[to], self.received.at[step - 1], g.at(to, g.lo), send_sem,
                   k.sem(f"{self.name}/recv"))
        k.later(self.received, send_sem, g.pair())

    def finish(self):
        g, k = self.group, self.links
        k.wait_recv(self.received, k.sem(f"{self.name}/recv"), g.pair())
        total = self.part[g.hi, g.lo].astype(F32) + self.from_pair[g.hi].astype(F32)
        for step in range(3):
            total = total + self.received[step].astype(F32)
        return total


class DirectScatter:
    def __init__(self, links, group, name, part, from_pair, pair_sum, received):
        self.links, self.group, self.name, self.part, self.received = links, group, name, part, received

    def send(self):
        g, k = self.group, self.links
        send_sem = k.sem(f"{self.name}/send")
        for step in SEND_ORDER:
            to = (g.index + step) % 8
            k.send(self.part.at[to // 2, to % 2], self.received.at[step - 1], g.member(to), send_sem,
                   k.sem(f"{self.name}/recv"))
        k.later(self.received, send_sem, g.pair())

    def middle(self):
        return
        yield

    def finish(self):
        g, k = self.group, self.links
        k.wait_recv(self.received, k.sem(f"{self.name}/recv"), g.pair())
        total = self.part[g.hi, g.lo].astype(F32)
        for step in range(7):
            total = total + self.received[step].astype(F32)
        return total


class PairGather:
    def __init__(self, links, group, name, whole, seven):
        self.links, self.group, self.name, self.whole = links, group, name, whole

    def send(self):
        g, k = self.group, self.links
        own = self.whole.at[g.hi, g.lo]
        send_sem = k.sem(f"{self.name}/send")
        for step in (2, 1, 3):
            k.send(own, own, g.at((g.hi + step) % 4, g.lo), send_sem, k.sem(f"{self.name}/recv", step - 1, 3))
        k.send(own, own, g.pair(), send_sem, k.sem(f"{self.name}/pair_recv"))
        k.later(self.whole.at[:, g.lo], send_sem, g.pair())

    def forward(self):
        g, k = self.group, self.links
        send_sem = k.sem(f"{self.name}/on_send")
        yield
        for step in (1, 3, 2):
            block = self.whole.at[(g.hi + 4 - step) % 4, g.lo]
            k.wait_recv(block, k.sem(f"{self.name}/recv", step - 1, 3), g.pair())
            k.send(block, block, g.pair(), send_sem, k.sem(f"{self.name}/pair_recv"))
        k.later(self.whole.at[pl.ds(0, 3), g.lo], send_sem, g.pair())

    def ready(self):
        g, k = self.group, self.links
        k.wait_recv(self.whole.at[:, 1 - g.lo], k.sem(f"{self.name}/pair_recv"), g.pair())


class DirectGather:
    def __init__(self, links, group, name, whole, seven):
        self.links, self.group, self.name, self.whole, self.seven = links, group, name, whole, seven

    def send(self):
        g, k = self.group, self.links
        own = self.whole.at[g.hi, g.lo]
        send_sem = k.sem(f"{self.name}/send")
        for step in SEND_ORDER:
            k.send(own, own, g.member((g.index + step) % 8), send_sem, k.sem(f"{self.name}/recv"))
        k.later(self.seven, send_sem, g.pair())

    def forward(self):
        return
        yield

    def ready(self):
        self.links.wait_recv(self.seven, self.links.sem(f"{self.name}/recv"), self.group.pair())


class Cross:
    def __init__(self, links, group, name, whole, partners):
        self.links, self.group, self.name, self.whole, self.partners = links, group, name, whole, partners

    def send(self, source, four):
        g, k = self.group, self.links
        send_sem = k.sem(f"{self.name}/send")
        for to in self.partners:
            k.send(source, self.whole.at[g.hi, g.lo], to, send_sem, k.sem(f"{self.name}/recv", g.hi, 4))
        k.later(four, send_sem, g.pair())

    def receive(self):
        g, k = self.group, self.links
        send_sem = k.sem(f"{self.name}/on_send")
        yield
        for hi in range(4):
            block = self.whole.at[hi, g.lo]
            k.wait_recv(block, k.sem(f"{self.name}/recv", hi, 4), g.pair())
            k.send(block, block, g.pair(), send_sem, k.sem(f"{self.name}/pair_recv"))
        k.later(self.whole.at[:, g.lo], send_sem, g.pair())

    def ready(self):
        g, k = self.group, self.links
        k.wait_recv(self.whole.at[:, 1 - g.lo], k.sem(f"{self.name}/pair_recv"), g.pair())


def exchange(links, group, name, table, combine):
    send_sem, recv_sem = links.sem(f"{name}/send"), links.sem(f"{name}/recv")
    for step in SEND_ORDER:
        links.send(table.at[0], table.at[step], group.member((group.index + step) % 8), send_sem, recv_sem)
    links.later(table.at[pl.ds(1, 7)], send_sem, group.pair())
    yield
    links.wait_recv(table.at[pl.ds(1, 7)], recv_sem, group.pair())
    return combine([table[k] for k in range(8)])


def pairwise(links, group, name, table, combine):
    pair_send, pair_recv = links.sem(f"{name}/pair_send"), links.sem(f"{name}/pair_recv")
    links.send(table.at[0], table.at[1], group.pair(), pair_send, pair_recv)
    links.later(table.at[0], pair_send, group.pair())
    yield
    links.wait_recv(table.at[1], pair_recv, group.pair())
    table[2] = combine([table[0], table[1]])
    send_sem, recv_sem = links.sem(f"{name}/send"), links.sem(f"{name}/recv")
    for step in (2, 1, 3):
        links.send(table.at[2], table.at[2 + step], group.at((group.hi + step) % 4, group.lo), send_sem, recv_sem)
    links.later(table.at[pl.ds(3, 3)], send_sem, group.pair())
    yield
    links.wait_recv(table.at[pl.ds(3, 3)], recv_sem, group.pair())
    return combine([table[k] for k in range(2, 6)])


def drive(chains, lead=0):
    alive = list(chains)
    if lead:
        for chain in alive:
            next(chain)
    for _ in range(lead):
        next(alive[0])
    while alive:
        for chain in list(alive):
            try:
                next(chain)
            except StopIteration:
                alive.remove(chain)


def add_all(parts):
    return functools.reduce(lambda left, right: left + right, parts)


def join_moments(parts):
    averages = [part[:, 0:1] for part in parts]
    average = add_all(averages) / len(parts)
    squares = add_all([part[:, 64:65] for part in parts])
    spread = add_all([(one - average) * (one - average) for one in averages])
    return two_lanes(average, squares + (MODEL if len(parts) == 2 else 2 * MODEL) * spread)


def two_lanes(first, second):
    lane = lax.broadcasted_iota(jnp.int32, (BLOCK, 128), 1)
    return jnp.where(lane < 64, first, second)


def local_moments(values):
    average = jnp.sum(values, 1, keepdims=True) / MODEL
    centered = values - average
    return two_lanes(average, jnp.sum(centered * centered, 1, keepdims=True))


def row_stats(joined):
    return two_lanes(joined[:, 0:1], lax.rsqrt(joined[:, 64:65] / D + epsilon))


def selection(rows, columns, source):
    row = lax.broadcasted_iota(jnp.int32, (rows, columns), 0)
    column = lax.broadcasted_iota(jnp.int32, (rows, columns), 1)
    return jnp.where(column == source(row), 1.0, 0.0)


WITHIN = BLOCK // 8


def swap_matrix():
    return selection(HALF, HALF, lambda i: ((i // WITHIN) % 8) * BLOCK + (i // BLOCK) * WITHIN + i % WITHIN).astype(BF16)


def pick_matrix(q):
    return selection(BLOCK, HALF, lambda i: (i // WITHIN) * BLOCK + q * WITHIN + i % WITHIN)


def halves_matrix():
    return selection(ROWS, ROWS, lambda i: ((i % BLOCK) // WITHIN) * 4 + (i // BLOCK) * WITHIN + i % WITHIN).astype(BF16)


def whole_matrix():
    return selection(ROWS, ROWS, lambda i: ((i % 4) // WITHIN) * BLOCK + (i // 4) * WITHIN + i % WITHIN).astype(BF16)


def moved(matrix, rows):
    return jnp.dot(matrix, rows, preferred_element_type=F32).astype(BF16)


def transpose_into(target, source):
    rows, columns = source.shape

    @pl.loop(0, rows // 512)
    def _(i):
        at = pl.ds(pl.multiple_of(i * 512, 512), 512)
        for j in range(0, columns, 512):
            target[pl.ds(j, 512), at] = source[at, pl.ds(j, 512)].T


def product(x, w_ref, transposed, k0, depth, n0, width):
    if transposed:
        return lax.dot_general(
            x, w_ref[pl.ds(n0, width), pl.ds(k0, depth)], (((1,), (1,)), ((), ())),
            preferred_element_type=F32,
        )
    return jnp.dot(x, w_ref[pl.ds(k0, depth), pl.ds(n0, width)], preferred_element_type=F32)


def kernel(
    tokens, out_grad, gain, shift, up, up_bias, down, down_bias, out_ref, grad_ref,
    U, V, W, gain_row, shift_row, up_row, down_row, raw, xall, xn, xn2, part, from_pair, pair_sum, received,
    hall, acc, part_m, from_pair_m, pair_sum_m, received_m, pre, hidden_grad, moments, stats, cross_stats,
    sendbuf, gradbuf, y0_own, own_stats, sems, local_sems,
):
    s, d, t = lax.axis_index("section"), lax.axis_index("dp"), lax.axis_index("tensor")

    barrier = pltpu.get_barrier_semaphore()
    greeted = [(s, d + 1 - 2 * (d % 2), t), (1 - s, d, t)]
    greeted += [(s, (d + 2 * k) % 8, t) for k in range(1, 4)]
    greeted += [(s, d, (t + k) % 8) for k in range(1, 8)]
    for to in greeted:
        pl.semaphore_signal(barrier, inc=1, device_id=to, device_id_type=MESH)

    def fetch(src, dst, index):
        copy = pltpu.make_async_copy(src, dst, local_sems.at[index])
        copy.start()
        return copy

    def branch(section):
        first = section == 0
        links = Links(sems)
        hidden_group = Group(section, "dp" if first else "tensor", d, t)
        model_group = Group(section, "tensor" if first else "dp", d, t)
        width_index, unit_index = (d, t) if first else (t, d)
        features = pl.ds(pl.multiple_of(width_index * MODEL, MODEL), MODEL)
        units = pl.ds(pl.multiple_of(unit_index * UNITS, UNITS), UNITS)
        g, hg = model_group, hidden_group
        get_own = fetch(tokens if first else out_grad, raw, 0)
        weights = [(up.at[0], U, 1), (down.at[0], V, 2)]
        gets = {}
        for src, dst, index in weights if first else weights[::-1]:
            gets[index] = fetch(src, dst, index)
        small = [
            fetch(gain.at[:, features], gain_row, 3), fetch(shift.at[:, features], shift_row, 4),
            fetch(up_bias.at[:, units], up_row, 5), fetch(down_bias.at[:, features], down_row, 6),
        ]

        def need(index):
            if index in gets:
                gets.pop(index).wait()

        get_own.wait()
        own_rows = moved(halves_matrix(), raw[...]) if HALVES == 2 else raw[...]
        for h in range(HALVES):
            xall[0, h, g.hi, g.lo] = own_rows[h * BLOCK:(h + 1) * BLOCK]
        def own_x(h):
            return xall[0, h, g.hi, g.lo].astype(F32)

        if first:
            for h in range(HALVES):
                moments[h, 0, 0] = local_moments(own_x(h))
        for copy in small:
            copy.wait()
        pl.semaphore_wait(barrier, len(greeted))

        def scatter_of(group):
            return PairScatter if group.axis == "dp" else DirectScatter

        def gather_of(group):
            return PairGather if group.axis == "dp" else DirectGather

        def scatter_hidden(slot, h):
            return [
                scatter_of(hg)(links, hg, f"h{slot}{h}{c}", part.at[slot, h, c], from_pair.at[slot, h, c],
                               pair_sum.at[slot, h, c], received.at[slot, h, c])
                for c in range(N_CHUNKS)
            ]

        def scatter_model(slot, h):
            return [
                scatter_of(g)(links, g, f"m{slot}{h}{m}", part_m.at[slot, h, m], from_pair_m.at[slot, h, m],
                              pair_sum_m.at[slot, h, m], received_m.at[slot, h, m])
                for m in range(M_CHUNKS)
            ]

        def gather_hidden(slot, h):
            return [gather_of(hg)(links, hg, f"g{slot}{h}{c}", hall.at[slot, h, c], received.at[slot, h, c]) for c in range(N_CHUNKS)]

        def gather_rows(name, slot, h):
            return gather_of(g)(links, g, f"{name}{h}", xall.at[slot, h], received_m.at[slot, h, 0])

        def start_hidden(x_ref, w_ref, transposed, scatters):
            for c, scatter in enumerate(scatters):
                x = x_ref[...].reshape(HALF, MODEL)
                for at in range(0, N_WIDTH, 512):
                    value = product(x, w_ref, transposed, 0, MODEL, c * N_WIDTH + at, 512)
                    scatter.part[:, :, :, pl.ds(at, 512)] = value.astype(BF16).reshape(4, 2, BLOCK, 512)
                scatter.send()
                yield from scatter.middle()

        def to_model(h, gathers, w_ref, transposed, scatters):
            for c, gather in enumerate(gathers):
                yield
                gather.ready()
                x = gather.whole[...].reshape(HALF, N_WIDTH)
                if c < N_CHUNKS - 1:
                    for at in range(0, MODEL, 512):
                        value = product(x, w_ref, transposed, c * N_WIDTH, N_WIDTH, at, 512)
                        acc[h, :, pl.ds(at, 512)] = value if c == 0 else acc[h, :, pl.ds(at, 512)] + value
                    continue
                for m, scatter in enumerate(scatters):
                    for at in range(0, M_WIDTH, 512):
                        value = product(x, w_ref, transposed, c * N_WIDTH, N_WIDTH, m * M_WIDTH + at, 512)
                        if c > 0:
                            value = value + acc[h, :, pl.ds(m * M_WIDTH + at, 512)]
                        scatter.part[:, :, :, pl.ds(at, 512)] = value.astype(BF16).reshape(4, 2, BLOCK, 512)
                    scatter.send()
                    if m >= 1:
                        yield from scatters[m - 1].middle()
            yield from scatters[-1].middle()

        def through(h, scatters, gathers, epilogue, w_ref, transposed, scatters_out):
            for c, scatter in enumerate(scatters):
                yield
                value = epilogue(h, unit_slice(c), scatter.finish())
                gathers[c].whole[hg.hi, hg.lo] = value.astype(BF16)
                gathers[c].send()
                if c >= 1:
                    yield from gathers[c - 1].forward()
            yield from gathers[-1].forward()
            yield from to_model(h, gathers, w_ref, transposed, scatters_out)

        def finish_model(scatters):
            yield
            return jnp.concatenate([scatter.finish() for scatter in scatters], axis=1)

        def normalize_all(h, source):
            for hi in range(4):
                for lo in range(2):
                    average = stats[h, hi, lo][:, 0:1]
                    inverse_dev = stats[h, hi, lo][:, 64:65]
                    unit = (source[hi, lo].astype(F32) - average) * inverse_dev
                    xn[h, hi, lo] = (unit * gain_row[...] + shift_row[...]).astype(BF16)

        def swapped(h, source):
            rows = moved(swap_matrix(), source[...].reshape(HALF, MODEL))
            xn2[h] = rows.reshape(4, 2, BLOCK, MODEL)

        def unit_slice(c):
            return pl.ds(c * N_WIDTH, N_WIDTH)

        def input_gradient(h, incoming, norm_grad, rows):
            average, inverse_dev = own_stats[h][:, 0:1], own_stats[h][:, 64:65]
            unit = (rows - average) * inverse_dev
            scaled = norm_grad * gain_row[...]
            table = moments.at[h, 2]
            table[0] = two_lanes(jnp.sum(scaled, 1, keepdims=True), jnp.sum(scaled * unit, 1, keepdims=True))
            total = yield from (pairwise if first else exchange)(links, hg, f"sums{h}", table, add_all)
            first_mean, second_mean = total[:, 0:1] / D, total[:, 64:65] / D
            return (incoming + inverse_dev * (scaled - first_mean - unit * second_mean)).astype(BF16)

        def store_rows(ref, rows):
            rows = rows[...].reshape(ROWS, MODEL)
            ref[0] = moved(whole_matrix(), rows) if HALVES == 2 else rows

        partners = [(1, 2 * k + t % 2, d) for k in range(4)]

        def y0_cross(h):
            return Cross(links, g, f"y0{h}", xall.at[1, h], partners)

        def stats_sems(h):
            return links.sem(f"y0stats{h}/send"), links.sem(f"y0stats{h}/recv")

        def transposed_sems(h):
            return links.sem(f"g1{h}/send"), links.sem(f"g1{h}/recv")

        def forward_chain(h):
            gather = gather_rows("x", 0, h)
            gather.send()
            joined = yield from pairwise(links, hg, f"first{h}", moments.at[h, 0], join_moments)
            own_stats[h] = row_stats(joined)
            stats[h, g.hi, g.lo] = own_stats[h]
            stats_gather = DirectGather(links, g, f"st{h}", stats.at[h], moments.at[h, 0, pl.ds(0, 7)])
            stats_gather.send()
            yield
            gather.ready()
            stats_gather.ready()
            normalize_all(h, xall.at[0, h])
            need(1)
            scatters = scatter_hidden(0, h)
            yield from start_hidden(xn.at[h], U, False, scatters)
            need(2)

            def forward_hidden(h, at, value):
                value = value + up_row[:, at]
                pre[h, :, at] = value
                return gelu_value(value)

            scatters_out = scatter_model(0, h)
            yield from through(h, scatters, gather_hidden(0, h), forward_hidden, V, False, scatters_out)
            mixed = yield from finish_model(scatters_out)
            y0 = (own_x(h) + mixed + down_row[...]).astype(BF16)
            sendbuf[0, h] = y0
            y0_cross(h).send(sendbuf.at[0, h], sendbuf.at[pl.ds(0, 4), h])
            moments[h, 1, 0] = local_moments(y0.astype(F32))
            joined = yield from pairwise(links, hg, f"second{h}", moments.at[h, 1], join_moments)
            cross_stats[h, 0] = row_stats(joined)
            send_sem, recv_sem = stats_sems(h)
            for q in range(8):
                links.send(cross_stats.at[h, 0], stats.at[h, g.hi, g.lo], (1, q, d), send_sem, recv_sem)
            links.later(cross_stats.at[h], send_sem, g.pair())

        def backward_chain(h):
            yield
            place = xall.at[1, h, g.hi, g.lo]
            links.wait_recv(place, transposed_sems(h)[1], g.pair())
            gather = gather_rows("g1x", 1, h)
            gather.send()
            yield
            gather.ready()
            swapped(h, xall.at[1, h])
            scatters = scatter_hidden(1, h)
            yield from start_hidden(xn2.at[h], U, False, scatters)

            def backward_hidden(h, at, value):
                return value * gelu_slope(pre[h, :, at])

            scatters_out = scatter_model(1, h)
            yield from through(h, scatters, gather_hidden(1, h), backward_hidden, W, False, scatters_out)
            norm_grad = yield from finish_model(scatters_out)
            incoming = xn2[h, g.hi, g.lo].astype(F32)
            gradbuf[h] = yield from input_gradient(h, incoming, norm_grad, own_x(h))

        def early_chain(h):
            gather = gather_rows("x", 0, h)
            gather.send()
            yield from gather.forward()
            yield
            gather.ready()
            need(2)
            scatters = scatter_hidden(0, h)
            yield from start_hidden(xall.at[0, h], V, True, scatters)
            for c in range(N_CHUNKS):
                yield
                hidden_grad[h, :, unit_slice(c)] = scatters[c].finish()

        def main_chain(h):
            rows = y0_cross(h)
            yield from rows.receive()
            yield
            rows.ready()
            links.wait_recv(stats.at[h], stats_sems(h)[1], g.pair())
            normalize_all(h, xall.at[1, h])
            swapped(h, xn.at[h])
            need(1)
            scatters = scatter_hidden(1, h)
            yield from start_hidden(xn2.at[h], U, False, scatters)
            pick = pick_matrix(d)
            y0_own[h] = jnp.dot(pick.astype(BF16), xall[1, h].reshape(HALF, MODEL), preferred_element_type=F32)
            own_stats[h] = jnp.dot(
                pick, stats[h].reshape(HALF, 128), preferred_element_type=F32, precision=lax.Precision.HIGHEST
            )

            def backward_hidden(h, at, value):
                value = value + up_row[:, at]
                pre[h, :, at] = value
                return hidden_grad[h, :, at] * gelu_slope(value)

            gathers = [
                PairGather(links, hg, f"g0{h}{c}", hall.at[0, h, c], None) for c in range(N_CHUNKS)
            ]
            scatters_out = scatter_model(0, h)
            yield from through(h, scatters, gathers, backward_hidden, W, False, scatters_out)
            norm_grad = yield from finish_model(scatters_out)
            gradbuf[h] = yield from input_gradient(h, own_x(h), norm_grad, y0_own[h])
            send_sem, recv_sem = transposed_sems(h)
            links.send(gradbuf.at[h], xall.at[1, h, g.hi, g.lo], (0, t, d), send_sem, recv_sem)
            links.later(gradbuf.at[h], send_sem, g.pair())

        def late_chain(h):
            gathers = gather_hidden(1, h)
            for c, gather in enumerate(gathers):
                gather.whole[hg.hi, hg.lo] = gelu_value(pre[h, :, unit_slice(c)]).astype(BF16)
                gather.send()
            scatters_out = scatter_model(1, h)
            yield from to_model(h, gathers, V, False, scatters_out)
            mixed = yield from finish_model(scatters_out)
            sendbuf[0, h] = (y0_own[h] + mixed + down_row[...]).astype(BF16)

        if first:
            drive([forward_chain(h) for h in range(HALVES)], FORWARD_LEAD)
            store_rows(out_ref, sendbuf.at[0])
            transpose_into(W, U)
            transpose_into(U, V)
            links.finish()
            drive([backward_chain(h) for h in range(HALVES)], BACKWARD_LEAD)
            store_rows(grad_ref, gradbuf)
        else:
            drive([early_chain(h) for h in range(HALVES)])
            links.finish()
            need(1)
            transpose_into(W, U)
            drive([main_chain(h) for h in range(HALVES)], MAIN_LEAD)
            store_rows(grad_ref, gradbuf)
            drive([late_chain(h) for h in range(HALVES)])
            store_rows(out_ref, sendbuf.at[0])
        links.finish()

    for section in range(2):
        pl.when(s == section)(functools.partial(branch, section))
    assert sum(width for _, width in SEM_NAMES.values()) <= SEM_COUNT


def hand_over(out, grad, out_ref, grad_ref):
    out_ref[...] = out[...]
    grad_ref[...] = grad[...]


def shards(tokens, out_grad, norm_gain, norm_shift, up_weight, up_bias, down_weight, down_bias):
    vmem = pltpu.VMEM
    hidden, model = (2, HALVES, N_CHUNKS), (2, HALVES, M_CHUNKS)
    results = pl.pallas_call(
        kernel,
        out_shape=[jax.ShapeDtypeStruct((1, ROWS, MODEL), BF16)] * 2,
        in_specs=[pl.BlockSpec(memory_space=pl.ANY)] * 8,
        out_specs=[pl.BlockSpec(memory_space=vmem)] * 2,
        scratch_shapes=[
            vmem((MODEL, UNITS), BF16),
            vmem((UNITS, MODEL), BF16),
            vmem((UNITS, MODEL), BF16),
            vmem((1, MODEL), F32),
            vmem((1, MODEL), F32),
            vmem((1, UNITS), F32),
            vmem((1, MODEL), F32),
            vmem((ROWS, MODEL), BF16),
            vmem((2, HALVES, 4, 2, BLOCK, MODEL), BF16),
            vmem((HALVES, 4, 2, BLOCK, MODEL), BF16),
            vmem((HALVES, 4, 2, BLOCK, MODEL), BF16),
            vmem(hidden + (4, 2, BLOCK, N_WIDTH), BF16),
            vmem(hidden + (4, BLOCK, N_WIDTH), BF16),
            vmem(hidden + (4, BLOCK, N_WIDTH), BF16),
            vmem(hidden + (7, BLOCK, N_WIDTH), BF16),
            vmem(hidden + (4, 2, BLOCK, N_WIDTH), BF16),
            vmem((HALVES, HALF, MODEL), F32),
            vmem(model + (4, 2, BLOCK, M_WIDTH), BF16),
            vmem(model + (4, BLOCK, M_WIDTH), BF16),
            vmem(model + (4, BLOCK, M_WIDTH), BF16),
            vmem(model + (7, BLOCK, M_WIDTH), BF16),
            vmem((HALVES, BLOCK, UNITS), F32),
            vmem((HALVES, BLOCK, UNITS), F32),
            vmem((HALVES, 3, 8, BLOCK, 128), F32),
            vmem((HALVES, 4, 2, BLOCK, 128), F32),
            vmem((HALVES, 8, BLOCK, 128), F32),
            vmem((4, HALVES, BLOCK, MODEL), BF16),
            vmem((HALVES, BLOCK, MODEL), BF16),
            vmem((HALVES, BLOCK, MODEL), F32),
            vmem((HALVES, BLOCK, 128), F32),
            pltpu.SemaphoreType.DMA((SEM_COUNT,)),
            pltpu.SemaphoreType.DMA((8,)),
        ],
        compiler_params=pltpu.CompilerParams(
            collective_id=0, has_side_effects=True, vmem_limit_bytes=58 * 2**20
        ),
        cost_estimate=pl.CostEstimate(flops=10**10, bytes_accessed=2 * 10**7, transcendentals=10**5),
        name="relay",
    )(tokens, out_grad, norm_gain, norm_shift, up_weight, up_bias, down_weight, down_bias)
    return pl.pallas_call(
        hand_over,
        out_shape=[jax.ShapeDtypeStruct((1, ROWS, MODEL), BF16)] * 2,
        in_specs=[pl.BlockSpec(memory_space=vmem)] * 2,
        out_specs=[pl.BlockSpec(memory_space=vmem)] * 2,
        name="hand_over",
    )(*results)


def solution(mesh):
    placed = (
        P("tensor", "dp"),
        P("tensor", "dp"),
        P("section", None),
        P("section", None),
        P("section", "dp", "tensor"),
        P("section", None),
        P("section", "tensor", "dp"),
        P("section", None),
    )
    return jax.shard_map(
        shards,
        mesh=mesh,
        in_specs=placed,
        out_specs=(P("section", "tensor", "dp"), P("section", "tensor", "dp")),
        check_vma=False,
    )
```
